32 devices in a mesh: lon: 8 (over y, x, core), head: 4 (over z).
Axes of the slice: x: 2, y: 2, z: 4, core: 2. Of those that a mesh axis runs over, the one named last changes fastest.
Arguments:
- activations: bfloat16 [16384, 1024], P('lon')
- qkv_weight: bfloat16 [1024, 3072], P(None, 'head'), may hold values from -0.1875 to 0.1875
- attn_grad: bfloat16 [16384, 1024], P('lon', 'head'), may hold values from -6 to 6
- pos_bias: float32 [16, 128, 128], P('head'), may hold values from -4 to 4
- key_counts: int32 [128], P('lon'), may hold values from 32 to 128, as said below
Outputs:
- input_grad: bfloat16 [16384, 1024], P(('lon', 'head'))
- weight_grad: float32 [1024, 3072], P(None, 'head')
The draws below stay inside these ranges and needn't reach their ends.
Inputs may be any that keep to these rules, and one draw needn't show every extreme that they name: key_counts[g] is the number of valid keys of shifted window g; windows of window row 0 and of the last window row may hold fewer than 128, all others hold 128.
All inputs are finite; a program needn't handle non-finite values.
Results may differ from the reference program's by a relative error of at most 0.019.
The reference program's roundings to bfloat16 on the way (of `projected` and `grad_proj`) count: a program that leaves them out, or rounds other values in their place, can miss the bound.
Values may be sent and summed in bfloat16 or wider, within the bound.
No kernel may reach another device: no remote copies, remote signals or barrier semaphores. Data moves between devices by JAX's collectives and lax.ppermute only.
A program may use at most 64 MiB of HBM per device.

```python
import math
import jax
import jax.numpy as jnp
from jax import lax

D = 1024
HEADS = 16
HEAD_DIM = 64
WIN = 128
WIN_ROWS = 8
WIN_COLS = 2
TOKENS = 16384
WINDOWS = 128
N_LON = 8
N_HEAD = 4


def draw_activations(key, part):
    first_key, second_key = jax.random.split(jax.random.fold_in(key, 11))
    values = jax.random.normal(first_key, (TOKENS, D), jnp.float32)
    scales = jnp.exp(jax.random.uniform(second_key, (TOKENS, 1), jnp.float32, math.log(0.5), math.log(2.0)))
    return jnp.clip(values * scales, -12.0, 12.0).astype(jnp.bfloat16)


def draw_key_counts(key, part):
    index = jnp.arange(WINDOWS, dtype=jnp.int32)
    row_index = index // WIN_COLS % WIN_ROWS
    polar = (row_index == 0) | (row_index == WIN_ROWS - 1)
    drawn = jax.random.randint(jax.random.fold_in(key, 23), (WINDOWS,), WIN // 4, WIN + 1, dtype=jnp.int32)
    return jnp.where(polar, drawn, WIN).astype(jnp.int32)


def shard_levels(key, shape, pieces, least, high):
    loudness = 1.0
    for axis_at, parts in pieces:
        steps = jax.random.uniform(jax.random.fold_in(jax.random.fold_in(key, 6), axis_at), (parts,), jnp.float32, least / len(pieces), high / len(pieces))
        loudness = loudness * jnp.repeat(jnp.exp(steps), shape[axis_at] // parts).reshape((-1,) + (1,) * (len(shape) - 1 - axis_at))
    return loudness


def normal_values(key, extent, spread, limit, shards=(), held_as=jnp.bfloat16):
    values = spread * jax.random.normal(key, extent, jnp.float32)
    if shards:
        values = values * shard_levels(key, extent, shards, -0.22, 0.18)
    return jnp.clip(values, -limit, limit).astype(held_as)


def setup_inputs(seed: int = 0) -> dict:
    keys = jax.random.split(jax.random.key(seed), 6)
    activations = draw_activations(jax.random.fold_in(keys[5], 71), 0)
    qkv_weight = normal_values(keys[1], (D, HEADS * 3 * HEAD_DIM), D ** -0.5, 0.1875, ((1, 4),))
    attn_grad = normal_values(keys[2], (TOKENS, HEADS * HEAD_DIM), 1.0, 6.0, ((0, 8), (1, 4)))
    pos_bias = normal_values(keys[3], (HEADS, WIN, WIN), 1.0, 4.0, ((0, 4),), jnp.float32)
    key_counts = draw_key_counts(jax.random.fold_in(keys[5], 71), 0)
    return dict(activations=activations, qkv_weight=qkv_weight, attn_grad=attn_grad, pos_bias=pos_bias, key_counts=key_counts)


def assemble(block_grid, far_rows):
    half_len = block_grid.shape[3]
    first_part = block_grid[:, :, 1]
    second_part = jnp.concatenate([block_grid[:, 1:, 0], far_rows[:, None]], axis=1)
    return jnp.concatenate([first_part, second_part], axis=2)

def window_grads(proj_win, delta_win, pos_bias, valid_count):
    scale_factor = 1.0 / math.sqrt(proj_win.shape[-1])
    queries = proj_win[:, :, :, 0].astype(jnp.float32)
    keys_part = proj_win[:, :, :, 1].astype(jnp.float32)
    values_part = proj_win[:, :, :, 2].astype(jnp.float32)
    delta_full = delta_win.astype(jnp.float32)
    scores = jnp.einsum('nqhe,nkhe->nhqk', queries, keys_part) * scale_factor + pos_bias[None].astype(jnp.float32)
    positions = jnp.arange(proj_win.shape[1], dtype=jnp.int32)
    valid_keys = positions[None, :] < valid_count[:, None]
    scores = jnp.where(valid_keys[:, None, None, :], scores, -jnp.inf)
    row_max = lax.optimization_barrier(jnp.max(scores, axis=-1, keepdims=True))
    weights = jnp.exp(scores - row_max)
    probs = weights / lax.optimization_barrier(jnp.sum(weights, axis=-1, keepdims=True))
    grad_probs = jnp.einsum('nqhe,nkhe->nhqk', delta_full, values_part)
    grad_scores = probs * (grad_probs - lax.optimization_barrier(jnp.sum(probs * grad_probs, axis=-1, keepdims=True)))
    probs_low = probs.astype(jnp.bfloat16).astype(jnp.float32)
    grads_low = grad_scores.astype(jnp.bfloat16).astype(jnp.float32)
    grad_values = jnp.einsum('nhqk,nqhe->nkhe', probs_low, delta_full)
    grad_queries = jnp.einsum('nhqk,nkhe->nqhe', grads_low, keys_part) * scale_factor
    grad_keys = jnp.einsum('nhqk,nqhe->nkhe', grads_low, queries) * scale_factor
    return jnp.stack([grad_queries, grad_keys, grad_values], axis=3).astype(jnp.bfloat16)

def reference(activations, qkv_weight, attn_grad, pos_bias, key_counts):
    half_len = WIN // 2
    width_all = HEADS * 3 * HEAD_DIM
    projected = jnp.dot(activations, qkv_weight, preferred_element_type=jnp.float32).astype(jnp.bfloat16)
    proj_grid = projected.reshape(N_LON, WIN_ROWS, WIN_COLS, 2, half_len, width_all)
    delta_grid = attn_grad.reshape(N_LON, WIN_ROWS, WIN_COLS, 2, half_len, HEADS * HEAD_DIM)
    far_proj = jnp.roll(proj_grid[:, :, 0, 0], -1, axis=0)
    far_delta = jnp.roll(delta_grid[:, :, 0, 0], -1, axis=0)
    band_counts = key_counts.reshape(N_LON, WIN_ROWS * WIN_COLS)

    def one_band(items):
        block_grid, far_rows, delta_block, delta_far, valid_count = items
        proj_win = assemble(block_grid, far_rows).reshape(WIN_ROWS * WIN_COLS, WIN, HEADS, 3, HEAD_DIM)
        delta_win = assemble(delta_block, delta_far).reshape(WIN_ROWS * WIN_COLS, WIN, HEADS, HEAD_DIM)
        result = window_grads(proj_win, delta_win, pos_bias, valid_count)
        return result.reshape(WIN_ROWS, WIN_COLS, WIN, width_all)
    gradients = lax.map(one_band, (proj_grid, far_proj, delta_grid, far_delta, band_counts))
    leading = gradients[:, :, :, :half_len]
    trailing = gradients[:, :, :, half_len:]
    returned = jnp.roll(trailing[:, :, WIN_COLS - 1], 1, axis=0)
    first_halves = jnp.concatenate([returned[:, :, None], trailing[:, :, :WIN_COLS - 1]], axis=2)
    grad_proj = jnp.stack([first_halves, leading], axis=3).reshape(TOKENS, width_all)
    group_width = width_all // N_HEAD
    input_grad = jnp.zeros((TOKENS, D), jnp.float32)
    for group_index in range(N_HEAD):
        low_col = group_index * group_width
        partial_grad = lax.dot_general(grad_proj[:, low_col:low_col + group_width], qkv_weight[:, low_col:low_col + group_width], (((1,), (1,)), ((), ())), preferred_element_type=jnp.float32)
        input_grad = input_grad + lax.optimization_barrier(partial_grad.astype(jnp.bfloat16)).astype(jnp.float32)
    weight_grad = lax.dot_general(activations, grad_proj, (((0,), (0,)), ((), ())), preferred_element_type=jnp.float32) / math.sqrt(TOKENS)
    return (input_grad.astype(jnp.bfloat16), weight_grad)
```

```python
import functools
import math

import jax
import jax.numpy as jnp
from jax import lax
from jax.experimental import pallas as pl
from jax.experimental.pallas import tpu as pltpu
from jax.sharding import PartitionSpec as P

HEAD_DIM = 64
WIN = 128
WIN_ROWS = 8
WIN_COLS = 2
HALF = WIN // 2
BAND = WIN_ROWS * WIN_COLS * WIN
ROW = WIN_COLS * WIN
VMEM_BYTES = 48 * 1024 * 1024

INWARD = ((0, 1), (3, 2))
ACROSS = ((1, 2), (2, 1))
OUTWARD = ((1, 0), (2, 3))
ORDER = ((3, 2, 1, 0), (3, 2, 0, 1), (0, 1, 3, 2), (0, 1, 2, 3))


def passed_along(shard, axis, by):
    size = lax.axis_size(axis)
    return lax.ppermute(shard, axis, [(i, (i + by) % size) for i in range(size)])


def swapped(shard, bits):
    size = lax.axis_size("lon")
    return lax.ppermute(shard, "lon", [(i, i ^ bits) for i in range(size)])


def attend(proj, delta, bias_ref, counts):
    scale = 1.0 / math.sqrt(HEAD_DIM)
    lane = lax.broadcasted_iota(jnp.int32, (WIN, 2 * HEAD_DIM), 1)
    low = lane < HEAD_DIM
    key_at = lax.broadcasted_iota(jnp.int32, (2, WIN, WIN), 1)

    def both(pair):
        zero = jnp.zeros_like(pair)
        return jnp.concatenate([jnp.where(low, pair, zero), jnp.where(low, zero, pair)], axis=0)

    def rolled(x):
        return pltpu.roll(x, HEAD_DIM, 1)

    def dot(x, y, on):
        return lax.dot_general(x, y, ((on[0], on[1]), ((), ())), preferred_element_type=jnp.float32)

    pairs = proj.shape[1] // (6 * HEAD_DIM)
    biases = [
        jnp.stack([bias_ref[2 * p].T, bias_ref[2 * p + 1].T], axis=0) for p in range(pairs)
    ]
    rows = []
    for w in range(2):
        tiles = []
        valid = key_at < counts[w]
        for p in range(pairs):
            at = [
                proj[w * WIN : (w + 1) * WIN, p * 384 + i * 128 : p * 384 + (i + 1) * 128]
                for i in range(3)
            ]
            queries = jnp.where(low, at[0], at[1]).astype(jnp.bfloat16)
            keys = rolled(jnp.where(low, at[2], at[0])).astype(jnp.bfloat16)
            values = jnp.where(low, at[1], at[2]).astype(jnp.bfloat16)
            grads = delta[w * WIN : (w + 1) * WIN, p * 128 : (p + 1) * 128]
            two_queries, two_keys, two_values, two_grads = map(both, (queries, keys, values, grads))
            scores = dot(two_keys, queries, ((1,), (1,))).reshape(2, WIN, WIN) * scale + biases[p]
            grad_probs = dot(two_values, grads, ((1,), (1,))).reshape(2, WIN, WIN)
            scores = jnp.where(valid, scores, -jnp.inf)
            weights = jnp.exp(scores - jnp.max(scores, axis=1, keepdims=True))
            probs = weights * (1.0 / jnp.sum(weights, axis=1, keepdims=True))
            inner = jnp.sum(probs * grad_probs, axis=1, keepdims=True)
            grad_scores = probs * (grad_probs - inner)
            probs_low = probs.astype(jnp.bfloat16)
            grads_low = grad_scores.astype(jnp.bfloat16)
            probs_side = jnp.concatenate([probs_low[0], probs_low[1]], axis=1)
            grads_side = jnp.concatenate([grads_low[0], grads_low[1]], axis=1)
            grad_values = dot(probs_side, two_grads, ((1,), (0,)))
            grad_keys = rolled(dot(grads_side, two_queries, ((1,), (0,))) * scale)
            grad_queries = dot(grads_low.reshape(2 * WIN, WIN), two_keys, ((0,), (0,))) * scale
            tiles.append(jnp.where(low, grad_queries, grad_keys))
            tiles.append(jnp.where(low, grad_values, grad_queries))
            tiles.append(jnp.where(low, grad_keys, grad_values))
        rows.append(jnp.concatenate(tiles, axis=1).astype(jnp.bfloat16))
    return jnp.concatenate(rows, axis=0)


def chunk_kernel(column, block_ref, counts_ref, act_ref, delta_ref, *rest):
    if column:
        act_far_ref, delta_far_ref, *rest = rest
    weight_ref, bias_ref = rest[:2]
    part_ref, grad_ref = rest[-2:]

    def gathered(near_ref, far_ref):
        pieces = []
        for i in range(2):
            base = i * ROW + column * WIN + HALF
            if column:
                pieces += [near_ref[base : base + HALF, :], far_ref[i * HALF : (i + 1) * HALF, :]]
            else:
                pieces += [near_ref[base : base + WIN, :]]
        return jnp.concatenate(pieces, axis=0)

    rows = gathered(act_ref, act_far_ref if column else None)
    delta = gathered(delta_ref, delta_far_ref if column else None)
    weight = weight_ref[...]
    proj = jnp.dot(rows, weight, preferred_element_type=jnp.float32)
    first = block_ref[0] * 2 * WIN_COLS + column
    grads = attend(proj, delta, bias_ref, [counts_ref[first], counts_ref[first + WIN_COLS]])
    grad_ref[...] = grads
    part_ref[...] = lax.dot_general(
        grads, weight, (((1,), (1,)), ((), ())), preferred_element_type=jnp.float32
    ).astype(jnp.bfloat16)


def chunk(column, block, counts, act, delta, far, weight, bias, held):
    width, dim, delta_width = weight.shape[1], act.shape[1], delta.shape[1]
    blocked = lambda j, block_ref, counts_ref: (block_ref[0], 0)
    whole2 = lambda j, block_ref, counts_ref: (0, 0)
    whole3 = lambda j, block_ref, counts_ref: (0, 0, 0)
    operands = [act, delta]
    specs = [pl.BlockSpec((2 * ROW, dim), blocked), pl.BlockSpec((2 * ROW, delta_width), blocked)]
    if column:
        operands += list(far)
        specs += [pl.BlockSpec((WIN, dim), blocked), pl.BlockSpec((WIN, delta_width), blocked)]
    operands += [weight, bias]
    specs += [pl.BlockSpec(weight.shape, whole2), pl.BlockSpec(bias.shape, whole3)]
    aliases = {}
    if held is not None:
        aliases = {2 + len(operands): 1}
        operands.append(held)
        specs.append(pl.BlockSpec(memory_space=pl.ANY))
    tokens = 2 * WIN
    return pl.pallas_call(
        functools.partial(chunk_kernel, column),
        grid_spec=pltpu.PrefetchScalarGridSpec(
            num_scalar_prefetch=2,
            grid=(1,),
            in_specs=specs,
            out_specs=[pl.BlockSpec((tokens, dim), whole2), pl.BlockSpec((tokens, width), blocked)],
        ),
        out_shape=[
            jax.ShapeDtypeStruct((tokens, dim), jnp.bfloat16),
            jax.ShapeDtypeStruct((4 * tokens, width), jnp.bfloat16),
        ],
        input_output_aliases=aliases,
        compiler_params=pltpu.CompilerParams(vmem_limit_bytes=VMEM_BYTES),
        cost_estimate=pl.CostEstimate(
            flops=5_000_000_000, bytes_accessed=4_000_000, transcendentals=500_000
        ),
        name=f"chunk_{column}",
    )(block, counts, *operands)


def weight_kernel(core_ref, act_ref, far_ref, near_grad_ref, far_grad_ref, out_ref):
    near, mixed = [], []
    for r in range(WIN_ROWS):
        near.append(act_ref[r * ROW + HALF : r * ROW + HALF + WIN, :])
        mixed.append(act_ref[r * ROW + WIN + HALF : (r + 1) * ROW, :])
        mixed.append(far_ref[r * HALF : (r + 1) * HALF, :])
    over = (((0,), (0,)), ((), ()))
    total = lax.dot_general(
        jnp.concatenate(near, axis=0), near_grad_ref[...], over, preferred_element_type=jnp.float32
    )
    total += lax.dot_general(
        jnp.concatenate(mixed, axis=0), far_grad_ref[...], over, preferred_element_type=jnp.float32
    )
    out_ref[...] = total.astype(out_ref.dtype)


def weight_half(half, act, far, near_grad, far_grad, dtype):
    dim, width = act.shape[1], near_grad.shape[1]
    tile = 256
    steps = dim // 2 // tile
    column = lambda i, half_ref: (0, half_ref[0] * steps + i)
    whole = lambda i, half_ref: (0, 0)
    return pl.pallas_call(
        weight_kernel,
        grid_spec=pltpu.PrefetchScalarGridSpec(
            num_scalar_prefetch=1,
            grid=(steps,),
            in_specs=[
                pl.BlockSpec((act.shape[0], tile), column),
                pl.BlockSpec((far.shape[0], tile), column),
                pl.BlockSpec(near_grad.shape, whole),
                pl.BlockSpec(far_grad.shape, whole),
            ],
            out_specs=pl.BlockSpec((tile, width), lambda i, half_ref: (i, 0)),
        ),
        out_shape=jax.ShapeDtypeStruct((dim // 2, width), dtype),
        compiler_params=pltpu.CompilerParams(vmem_limit_bytes=VMEM_BYTES),
        cost_estimate=pl.CostEstimate(
            flops=2_000_000_000, bytes_accessed=8_000_000, transcendentals=0
        ),
        name="weight_half",
    )(half, act, far, near_grad, far_grad)


def split_kernel(chip_ref, mine_ref, theirs_ref, own_ref, *outs):
    rows = own_ref.shape[0]
    for bits in range(4):
        at = pl.ds(pl.multiple_of((chip_ref[0] ^ bits) * rows, rows), rows)
        total = mine_ref[at, :] + theirs_ref[at, :].astype(jnp.float32)
        if bits:
            outs[bits - 1][...] = total.astype(jnp.bfloat16)
        else:
            own_ref[...] = total


def join_kernel(scale, chip_ref, own_ref, a_ref, b_ref, c_ref, out_ref):
    total = own_ref[...] + a_ref[...].astype(jnp.float32)
    total = (total + b_ref[...].astype(jnp.float32)) + c_ref[...].astype(jnp.float32)
    out_ref[...] = (total * scale).astype(jnp.bfloat16)


def gather_kernel(chip_ref, own_ref, a_ref, b_ref, c_ref, out_ref):
    rows = own_ref.shape[0]
    for bits, ref in enumerate((own_ref, a_ref, b_ref, c_ref)):
        out_ref[pl.ds(pl.multiple_of((chip_ref[0] ^ bits) * rows, rows), rows), :] = ref[...]


def widen_kernel(core_ref, mine_ref, theirs_ref, out_ref):
    rows = mine_ref.shape[0]
    for other, ref in enumerate((mine_ref, theirs_ref)):
        at = pl.ds(pl.multiple_of((core_ref[0] ^ other) * rows, rows), rows)
        out_ref[at, :] = ref[...].astype(jnp.float32)


def small(kernel, out_shape, place, *operands):
    vmem = pl.BlockSpec(memory_space=pltpu.VMEM)
    several = isinstance(out_shape, list)
    return pl.pallas_call(
        kernel,
        in_specs=[pl.BlockSpec(memory_space=pltpu.SMEM)] + [vmem] * len(operands),
        out_specs=[vmem] * len(out_shape) if several else vmem,
        out_shape=out_shape,
        compiler_params=pltpu.CompilerParams(vmem_limit_bytes=VMEM_BYTES),
    )(place, *operands)


def summed_weight_grad(act, far, near_grad, far_grad, total_tokens):
    dim, width = act.shape[1], near_grad.shape[1]
    lon = lax.axis_index("lon")
    core, chip = (lon % 2).reshape(1), (lon // 2).reshape(1)
    outgoing = weight_half(1 - core, act, far, near_grad, far_grad, jnp.bfloat16)
    incoming = swapped(outgoing, 1)
    mine = weight_half(core, act, far, near_grad, far_grad, jnp.float32)
    block = (dim // 8, width)
    low = jax.ShapeDtypeStruct(block, jnp.bfloat16)
    own, *sent = small(
        split_kernel, [jax.ShapeDtypeStruct(block, jnp.float32), low, low, low], chip, mine, incoming
    )
    came = [swapped(part, 2 * (i + 1)) for i, part in enumerate(sent)]
    scale = 1.0 / math.sqrt(total_tokens)
    done = small(functools.partial(join_kernel, scale), low, chip, own, *came)
    others = [swapped(done, 2 * (i + 1)) for i in range(3)]
    half = jax.ShapeDtypeStruct((dim // 2, width), jnp.bfloat16)
    gathered = small(gather_kernel, half, chip, done, *others)
    other_half = swapped(gathered, 1)
    return small(
        widen_kernel, jax.ShapeDtypeStruct((dim, width), jnp.float32), core, gathered, other_half
    )


def add(*parts):
    total = parts[0].astype(jnp.float32)
    for part in parts[1:]:
        total = total + part.astype(jnp.float32)
    return total.astype(jnp.bfloat16)


def line_shards(activations, qkv_weight, attn_grad, pos_bias, key_counts):
    dim, delta_width = activations.shape[1], attn_grad.shape[1]
    total_tokens = activations.shape[0] * lax.axis_size("lon")

    def first_rows(x):
        return x.reshape(WIN_ROWS, ROW, x.shape[1])[:, :HALF].reshape(WIN_ROWS * HALF, x.shape[1])

    far = tuple(passed_along(first_rows(x), "lon", -1) for x in (activations, attn_grad))
    order = jnp.asarray(ORDER, jnp.int32)[lax.axis_index("head")]
    parts, held = [], []
    for column in range(2):
        here, grads = [], None
        for k in range(4):
            part, grads = chunk(
                column, order[k : k + 1], key_counts, activations, attn_grad, far, qkv_weight, pos_bias, grads
            )
            here.append(part)
        parts.append(here)
        held.append(grads)

    def hop(x, pairs):
        return lax.ppermute(x, "head", pairs)

    sums = []
    for here in parts:
        in_a = hop(here[0], INWARD)
        in_b = hop(here[1], INWARD)
        in_c = hop(here[2], INWARD)
        over_a = hop(add(here[0], in_a), ACROSS)
        over_b = hop(add(here[1], in_b), ACROSS)
        out = hop(add(here[2], over_a), OUTWARD)
        sums.append(add(here[3], in_c, over_b, out))
    near, mixed = (x.reshape(2, WIN, dim) for x in sums)
    back = passed_along(mixed[:, HALF:], "lon", 1)
    input_grad = jnp.concatenate([back, near, mixed[:, :HALF]], axis=1).reshape(2 * ROW, dim)
    weight_grad = summed_weight_grad(activations, far[0], held[0], held[1], total_tokens)
    return (input_grad, weight_grad)


def assemble(block_grid, far_rows):
    first_part = block_grid[:, :, 1]
    second_part = jnp.concatenate([block_grid[:, 1:, 0], far_rows[:, None]], axis=1)
    return jnp.concatenate([first_part, second_part], axis=2)


def window_grads(proj_win, delta_win, pos_bias, valid_count):
    scale_factor = 1.0 / math.sqrt(proj_win.shape[-1])
    queries = proj_win[:, :, :, 0]
    keys_part = proj_win[:, :, :, 1]
    values_part = proj_win[:, :, :, 2]
    scores = (
        jnp.einsum("nqhe,nkhe->nhqk", queries, keys_part, preferred_element_type=jnp.float32)
        * scale_factor
        + pos_bias[None]
    )
    positions = jnp.arange(proj_win.shape[1], dtype=jnp.int32)
    valid_keys = positions[None, :] < valid_count[:, None]
    scores = jnp.where(valid_keys[:, None, None, :], scores, -jnp.inf)
    row_max = jnp.max(scores, axis=-1, keepdims=True)
    weights = jnp.exp(scores - row_max)
    probs = weights / jnp.sum(weights, axis=-1, keepdims=True)
    grad_probs = jnp.einsum(
        "nqhe,nkhe->nhqk", delta_win, values_part, preferred_element_type=jnp.float32
    )
    grad_scores = probs * (grad_probs - jnp.sum(probs * grad_probs, axis=-1, keepdims=True))
    probs_low = probs.astype(jnp.bfloat16)
    grads_low = grad_scores.astype(jnp.bfloat16)
    grad_values = jnp.einsum(
        "nhqk,nqhe->nkhe", probs_low, delta_win, preferred_element_type=jnp.float32
    )
    grad_queries = (
        jnp.einsum("nhqk,nkhe->nqhe", grads_low, keys_part, preferred_element_type=jnp.float32)
        * scale_factor
    )
    grad_keys = (
        jnp.einsum("nhqk,nqhe->nkhe", grads_low, queries, preferred_element_type=jnp.float32)
        * scale_factor
    )
    return jnp.stack([grad_queries, grad_keys, grad_values], axis=3).astype(jnp.bfloat16)


def any_shards(activations, qkv_weight, attn_grad, pos_bias, key_counts):
    heads_here = pos_bias.shape[0]
    width_all = qkv_weight.shape[1]
    delta_width = attn_grad.shape[1]
    projected = jnp.dot(activations, qkv_weight, preferred_element_type=jnp.float32).astype(
        jnp.bfloat16
    )
    proj_grid = projected.reshape(WIN_ROWS, WIN_COLS, 2, HALF, width_all)
    delta_grid = attn_grad.reshape(WIN_ROWS, WIN_COLS, 2, HALF, delta_width)
    outgoing = jnp.concatenate([proj_grid[:, 0, 0], delta_grid[:, 0, 0]], axis=2)
    incoming = passed_along(outgoing, "lon", -1)
    proj_win = assemble(proj_grid, incoming[:, :, :width_all])
    delta_win = assemble(delta_grid, incoming[:, :, width_all:])
    gradients = window_grads(
        proj_win.reshape(WIN_ROWS * WIN_COLS, WIN, heads_here, 3, HEAD_DIM),
        delta_win.reshape(WIN_ROWS * WIN_COLS, WIN, heads_here, HEAD_DIM),
        pos_bias,
        key_counts,
    ).reshape(WIN_ROWS, WIN_COLS, WIN, width_all)
    leading = gradients[:, :, :HALF]
    trailing = gradients[:, :, HALF:]
    returned = passed_along(trailing[:, WIN_COLS - 1], "lon", 1)
    first_halves = jnp.concatenate([returned[:, None], trailing[:, : WIN_COLS - 1]], axis=1)
    grad_proj = jnp.stack([first_halves, leading], axis=2).reshape(BAND, width_all)
    local_grad = lax.dot_general(
        activations, grad_proj, (((0,), (0,)), ((), ())), preferred_element_type=jnp.float32
    )
    total_tokens = activations.shape[0] * lax.axis_size("lon")
    weight_grad = lax.psum(local_grad, "lon") / math.sqrt(total_tokens)
    partial_grad = lax.dot_general(
        grad_proj, qkv_weight, (((1,), (1,)), ((), ())), preferred_element_type=jnp.float32
    )
    partial_low = lax.optimization_barrier(partial_grad.astype(jnp.bfloat16)).astype(jnp.float32)
    input_grad = lax.psum_scatter(
        partial_low.astype(jnp.bfloat16), "head", scatter_dimension=0, tiled=True
    )
    return (input_grad, weight_grad)


def solution(mesh):
    placed = (P("lon", None), P(None, "head"), P("lon", "head"), P("head", None, None), P("lon"))
    on_line = mesh.shape["head"] == 4 and mesh.shape["lon"] == 8
    return jax.shard_map(
        line_shards if on_line else any_shards,
        mesh=mesh,
        in_specs=placed,
        out_specs=(P(("lon", "head"), None), P(None, "head")),
        check_vma=False,
    )
```

```python
import functools
import math

import jax
import jax.numpy as jnp
from jax import lax
from jax.experimental import pallas as pl
from jax.experimental.pallas import tpu as pltpu
from jax.sharding import PartitionSpec as P

HEAD_DIM = 64
WIN = 128
WIN_ROWS = 8
WIN_COLS = 2
HALF = WIN // 2
BAND = WIN_ROWS * WIN_COLS * WIN
ROW = WIN_COLS * WIN
VMEM_BYTES = 48 * 1024 * 1024

BESIDE, ACROSS = 1, 3
ORDER = (2, 1, 3, 0)
SMALL_COST = pl.CostEstimate(flops=1_000_000, bytes_accessed=100_000, transcendentals=0)


def passed_along(shard, axis, by):
    size = lax.axis_size(axis)
    return lax.ppermute(shard, axis, [(i, (i + by) % size) for i in range(size)])


def swapped(shard, bits):
    size = lax.axis_size("lon")
    return lax.ppermute(shard, "lon", [(i, i ^ bits) for i in range(size)])


def attend(proj, delta, bias_ref, counts):
    scale = 1.0 / math.sqrt(HEAD_DIM)
    lane = lax.broadcasted_iota(jnp.int32, (WIN, 2 * HEAD_DIM), 1)
    low = lane < HEAD_DIM
    key_at = lax.broadcasted_iota(jnp.int32, (2, WIN, WIN), 1)

    def both(pair):
        zero = jnp.zeros_like(pair)
        return jnp.concatenate([jnp.where(low, pair, zero), jnp.where(low, zero, pair)], axis=0)

    def rolled(x):
        return pltpu.roll(x, HEAD_DIM, 1)

    def dot(x, y, on):
        return lax.dot_general(x, y, ((on[0], on[1]), ((), ())), preferred_element_type=jnp.float32)

    pairs = proj.shape[1] // (6 * HEAD_DIM)
    biases = [bias_ref[2 * p : 2 * p + 2] for p in range(pairs)]
    rows = []
    for w in range(2):
        tiles = []
        valid = key_at < counts[w]
        for p in range(pairs):
            at = [
                proj[w * WIN : (w + 1) * WIN, p * 384 + i * 128 : p * 384 + (i + 1) * 128]
                for i in range(3)
            ]
            queries = jnp.where(low, at[0], at[1]).astype(jnp.bfloat16)
            keys = rolled(jnp.where(low, at[2], at[0])).astype(jnp.bfloat16)
            values = jnp.where(low, at[1], at[2]).astype(jnp.bfloat16)
            grads = delta[w * WIN : (w + 1) * WIN, p * 128 : (p + 1) * 128]
            two_queries, two_keys, two_values, two_grads = map(both, (queries, keys, values, grads))
            scores = dot(two_keys, queries, ((1,), (1,))).reshape(2, WIN, WIN) * scale + biases[p]
            grad_probs = dot(two_values, grads, ((1,), (1,))).reshape(2, WIN, WIN)
            scores = jnp.where(valid, scores, -jnp.inf)
            weights = jnp.exp(scores - jnp.max(scores, axis=1, keepdims=True))
            probs = weights * (1.0 / jnp.sum(weights, axis=1, keepdims=True))
            inner = jnp.sum(probs * grad_probs, axis=1, keepdims=True)
            grad_scores = probs * (grad_probs - inner)
            probs_low = probs.astype(jnp.bfloat16)
            grads_low = grad_scores.astype(jnp.bfloat16)
            probs_side = jnp.concatenate([probs_low[0], probs_low[1]], axis=1)
            grads_side = jnp.concatenate([grads_low[0], grads_low[1]], axis=1)
            grad_values = dot(probs_side, two_grads, ((1,), (0,)))
            grad_keys = rolled(dot(grads_side, two_queries, ((1,), (0,))) * scale)
            grad_queries = dot(grads_low.reshape(2 * WIN, WIN), two_keys, ((0,), (0,))) * scale
            tiles.append(jnp.where(low, grad_queries, grad_keys))
            tiles.append(jnp.where(low, grad_values, grad_queries))
            tiles.append(jnp.where(low, grad_keys, grad_values))
        rows.append(jnp.concatenate(tiles, axis=1).astype(jnp.bfloat16))
    return jnp.concatenate(rows, axis=0)


def block_at(head, step):
    bits = jnp.where(step == 3, ORDER[3], ORDER[2])
    bits = jnp.where(step == 1, ORDER[1], bits)
    return head ^ jnp.where(step == 0, ORDER[0], bits)


def pack_kernel(act_ref, delta_ref, out_ref, sems):
    dim = act_ref.shape[2]
    copies = [
        pltpu.make_async_copy(
            act_ref.at[:, pl.ds(0, HALF), :], out_ref.at[:, :, pl.ds(0, dim)], sems.at[0]
        ),
        pltpu.make_async_copy(
            delta_ref.at[:, pl.ds(0, HALF), :],
            out_ref.at[:, :, pl.ds(dim, delta_ref.shape[2])],
            sems.at[1],
        ),
    ]
    for copy in copies:
        copy.start()
    for copy in copies:
        copy.wait()


def first_rows(act, delta):
    dim, delta_width = act.shape[1], delta.shape[1]
    anywhere = pl.BlockSpec(memory_space=pl.ANY)
    return pl.pallas_call(
        pack_kernel,
        in_specs=[anywhere, anywhere],
        out_specs=pl.BlockSpec(memory_space=pltpu.VMEM),
        out_shape=jax.ShapeDtypeStruct((WIN_ROWS, HALF, dim + delta_width), act.dtype),
        scratch_shapes=[pltpu.SemaphoreType.DMA((2,))],
        name="first_rows",
    )(act.reshape(WIN_ROWS, ROW, dim), delta.reshape(WIN_ROWS, ROW, delta_width))


def turned_biases(bias_ref, turned_ref):
    @pl.when(pl.program_id(0) == 0)
    def _():
        for h in range(bias_ref.shape[0]):
            turned_ref[h] = bias_ref[h].T


def counts_of(counts_ref, block, column):
    first = block * 2 * WIN_COLS + column
    return [counts_ref[first], counts_ref[first + WIN_COLS]]


def part_of(grads, weight):
    return lax.dot_general(
        grads, weight, (((1,), (1,)), ((), ())), preferred_element_type=jnp.float32
    ).astype(jnp.bfloat16)


def near_kernel(
    start, steps, head_ref, counts_ref, act_ref, delta_ref, weight_ref, bias_ref, *rest
):
    outs, turned_ref = rest[-2 - steps : -1], rest[-1]
    turned_biases(bias_ref, turned_ref)
    at = [slice(i * ROW + HALF, i * ROW + HALF + WIN) for i in range(2)]
    rows = jnp.concatenate([act_ref[s, :] for s in at], axis=0)
    delta = jnp.concatenate([delta_ref[s, :] for s in at], axis=0)
    weight = weight_ref[...]
    proj = jnp.dot(rows, weight, preferred_element_type=jnp.float32)
    step = pl.program_id(0)
    counts = counts_of(counts_ref, block_at(head_ref[0], step + start), 0)
    grads = attend(proj, delta, turned_ref, counts)
    outs[-1][...] = grads
    part = part_of(grads, weight)
    for i in range(steps):

        @pl.when(step == i)
        def _():
            outs[i][...] = part


def near_windows(start, steps, head, counts, act, delta, weight, bias, held):
    width, dim, delta_width = weight.shape[1], act.shape[1], delta.shape[1]
    blocked = lambda j, head_ref, counts_ref: (block_at(head_ref[0], j + start), 0)
    whole2 = lambda j, head_ref, counts_ref: (0, 0)
    whole3 = lambda j, head_ref, counts_ref: (0, 0, 0)
    tokens = 2 * WIN
    operands = [act, delta, weight, bias]
    specs = [
        pl.BlockSpec((2 * ROW, dim), blocked),
        pl.BlockSpec((2 * ROW, delta_width), blocked),
        pl.BlockSpec(weight.shape, whole2),
        pl.BlockSpec(bias.shape, whole3),
    ]
    aliases = {}
    if held is not None:
        aliases = {2 + len(operands): steps}
        operands.append(held)
        specs.append(pl.BlockSpec(memory_space=pl.ANY))
    part = jax.ShapeDtypeStruct((tokens, dim), jnp.bfloat16)
    return pl.pallas_call(
        functools.partial(near_kernel, start, steps),
        grid_spec=pltpu.PrefetchScalarGridSpec(
            num_scalar_prefetch=2,
            grid=(steps,),
            in_specs=specs,
            out_specs=[pl.BlockSpec((tokens, dim), whole2)] * steps
            + [pl.BlockSpec((tokens, width), lambda j, head_ref, counts_ref: (j + start, 0))],
            scratch_shapes=[pltpu.VMEM(bias.shape, bias.dtype)],
        ),
        out_shape=[part] * steps + [jax.ShapeDtypeStruct((4 * tokens, width), jnp.bfloat16)],
        input_output_aliases=aliases,
        compiler_params=pltpu.CompilerParams(vmem_limit_bytes=VMEM_BYTES),
        cost_estimate=SMALL_COST,
        name="near_windows",
    )(head, counts, *operands)


def far_kernel(
    head_ref, core_ref, counts_ref, act_ref, delta_ref, far_ref, weight_ref, bias_ref, held_ref, *rest
):
    outs, send_ref, keep_ref, turned_ref, total_ref = rest[:8], *rest[8:]
    turned_biases(bias_ref, turned_ref)
    dim, delta_width = act_ref.shape[1], delta_ref.shape[1]
    step = pl.program_id(0)

    def mixed(near_ref, low, high):
        pieces = []
        for i in range(2):
            pieces.append(near_ref[(i + 1) * ROW - HALF : (i + 1) * ROW, :])
            pieces.append(far_ref[i * HALF : (i + 1) * HALF, low:high])
        return jnp.concatenate(pieces, axis=0)

    rows = mixed(act_ref, 0, dim)
    delta = mixed(delta_ref, dim, dim + delta_width)
    weight = weight_ref[...]
    proj = jnp.dot(rows, weight, preferred_element_type=jnp.float32)
    counts = counts_of(counts_ref, block_at(head_ref[0], step), 1)
    grads = attend(proj, delta, turned_ref, counts)
    part = part_of(grads, weight)
    for i in range(4):

        @pl.when(step == i)
        def _():
            for w in range(2):
                base = w * WIN
                outs[2 * i][w * HALF : (w + 1) * HALF, :] = part[base + HALF : base + WIN]
                outs[2 * i + 1][w * HALF : (w + 1) * HALF, :] = part[base : base + HALF]

    near_rows = [act_ref[i * ROW + HALF : i * ROW + HALF + WIN, :] for i in range(2)]
    all_rows = jnp.concatenate(near_rows + [rows], axis=0)
    all_grads = jnp.concatenate([held_ref[...], grads], axis=0)
    product = lax.dot_general(
        all_rows, all_grads, (((0,), (0,)), ((), ())), preferred_element_type=jnp.float32
    )

    @pl.when(step == 0)
    def _():
        total_ref[...] = product

    @pl.when(step > 0)
    def _():
        total_ref[...] += product

    @pl.when(step == 3)
    def _():
        half = dim // 2
        core = core_ref[0]
        keep_ref[...] = total_ref[pl.ds(pl.multiple_of(core * half, half), half), :]
        send_ref[...] = total_ref[pl.ds(pl.multiple_of((1 - core) * half, half), half), :].astype(
            jnp.bfloat16
        )


def far_windows(head, core, counts, act, delta, far, weight, bias, held):
    width, dim, delta_width = weight.shape[1], act.shape[1], delta.shape[1]
    blocked = lambda j, head_ref, core_ref, counts_ref: (block_at(head_ref[0], j), 0)
    whole2 = lambda j, head_ref, core_ref, counts_ref: (0, 0)
    whole3 = lambda j, head_ref, core_ref, counts_ref: (0, 0, 0)
    part = jax.ShapeDtypeStruct((WIN, dim), jnp.bfloat16)
    return pl.pallas_call(
        far_kernel,
        grid_spec=pltpu.PrefetchScalarGridSpec(
            num_scalar_prefetch=3,
            grid=(4,),
            in_specs=[
                pl.BlockSpec((2 * ROW, dim), blocked),
                pl.BlockSpec((2 * ROW, delta_width), blocked),
                pl.BlockSpec((WIN, dim + delta_width), blocked),
                pl.BlockSpec(weight.shape, whole2),
                pl.BlockSpec(bias.shape, whole3),
                pl.BlockSpec((2 * WIN, width), lambda j, head_ref, core_ref, counts_ref: (j, 0)),
            ],
            out_specs=[pl.BlockSpec((WIN, dim), whole2)] * 8
            + [pl.BlockSpec((dim // 2, width), whole2)] * 2,
            scratch_shapes=[
                pltpu.VMEM(bias.shape, bias.dtype),
                pltpu.VMEM((dim, width), jnp.float32),
            ],
        ),
        out_shape=[part] * 8
        + [
            jax.ShapeDtypeStruct((dim // 2, width), jnp.bfloat16),
            jax.ShapeDtypeStruct((dim // 2, width), jnp.float32),
        ],
        compiler_params=pltpu.CompilerParams(vmem_limit_bytes=VMEM_BYTES),
        cost_estimate=SMALL_COST,
        name="far_windows",
    )(head, core, counts, act, delta, far, weight, bias, held)


def split_kernel(chip_ref, mine_ref, theirs_ref, own_ref, *outs):
    rows = own_ref.shape[0]
    for bits in range(4):
        at = pl.ds(pl.multiple_of((chip_ref[0] ^ bits) * rows, rows), rows)
        total = mine_ref[at, :] + theirs_ref[at, :].astype(jnp.float32)
        if bits:
            outs[bits - 1][...] = total.astype(jnp.bfloat16)
        else:
            own_ref[...] = total


def join_kernel(scale, chip_ref, own_ref, a_ref, b_ref, c_ref, out_ref):
    total = own_ref[...] + a_ref[...].astype(jnp.float32)
    total = (total + b_ref[...].astype(jnp.float32)) + c_ref[...].astype(jnp.float32)
    out_ref[...] = (total * scale).astype(jnp.bfloat16)


def gather_kernel(chip_ref, own_ref, a_ref, b_ref, c_ref, out_ref):
    rows = own_ref.shape[0]
    for bits, ref in enumerate((own_ref, a_ref, b_ref, c_ref)):
        out_ref[pl.ds(pl.multiple_of((chip_ref[0] ^ bits) * rows, rows), rows), :] = ref[...]


def widen_kernel(core_ref, mine_ref, theirs_ref, out_ref):
    rows = mine_ref.shape[0]
    for other, ref in enumerate((mine_ref, theirs_ref)):
        at = pl.ds(pl.multiple_of((core_ref[0] ^ other) * rows, rows), rows)
        out_ref[at, :] = ref[...].astype(jnp.float32)


def small(kernel, out_shape, place, *operands):
    vmem = pl.BlockSpec(memory_space=pltpu.VMEM)
    several = isinstance(out_shape, list)
    return pl.pallas_call(
        kernel,
        in_specs=[pl.BlockSpec(memory_space=pltpu.SMEM)] + [vmem] * len(operands),
        out_specs=[vmem] * len(out_shape) if several else vmem,
        out_shape=out_shape,
        compiler_params=pltpu.CompilerParams(vmem_limit_bytes=VMEM_BYTES),
    )(place, *operands)


def after(x, *others):
    return lax.optimization_barrier((x, *others))[0]


def add(*parts):
    total = parts[0].astype(jnp.float32)
    for part in parts[1:]:
        total = total + part.astype(jnp.float32)
    return total.astype(jnp.bfloat16)


def line_shards(activations, qkv_weight, attn_grad, pos_bias, key_counts):
    dim, width = qkv_weight.shape
    total_tokens = activations.shape[0] * lax.axis_size("lon")
    head = lax.axis_index("head").reshape(1)
    lon = lax.axis_index("lon")
    core, chip = (lon % 2).reshape(1), (lon // 2).reshape(1)

    arrived = []

    def hop(x, bits):
        x = x if len(arrived) < 2 else after(x, arrived[-2])
        pairs = [(i, i ^ bits) for i in range(lax.axis_size("head"))]
        arrived.append(lax.ppermute(x, "head", pairs))
        return arrived[-1]

    far = passed_along(first_rows(activations, attn_grad), "lon", -1)
    here = (activations, attn_grad, qkv_weight, pos_bias)
    first, held = near_windows(0, 1, head, key_counts, *here, None)
    in_near = [hop(first, BESIDE)]
    *near, held = near_windows(1, 3, head, key_counts, *here, held)
    in_near.append(hop(near[0], BESIDE))
    in_near.append(hop(add(near[1], in_near[0]), ACROSS))
    far = after(far, in_near[0]).reshape(WIN_ROWS * HALF, far.shape[2])
    *parts, outgoing, mine = far_windows(
        head, core, key_counts, activations, attn_grad, far, qkv_weight, pos_bias, held
    )
    nexts, this = parts[0::2], parts[1::2]
    in_next, in_this = [hop(nexts[0], BESIDE)], [hop(this[0], BESIDE)]
    in_next.append(hop(add(nexts[2], in_next[0]), ACROSS))
    in_next.append(hop(nexts[1], BESIDE))
    in_this.append(hop(add(this[2], in_this[0]), ACROSS))
    in_this.append(hop(this[1], BESIDE))
    near_sum = add(near[2], *in_near[1:])
    back = passed_along(add(nexts[3], *in_next[1:]), "lon", 1)
    this_sum = add(this[3], *in_this[1:])
    input_grad = jnp.concatenate(
        [x.reshape(2, -1, dim) for x in (back, near_sum, this_sum)], axis=1
    ).reshape(2 * ROW, dim)

    incoming = swapped(outgoing, 1)
    block = (dim // 8, width)
    low = jax.ShapeDtypeStruct(block, jnp.bfloat16)
    own, *sent = small(
        split_kernel,
        [jax.ShapeDtypeStruct(block, jnp.float32), low, low, low],
        after(chip, *in_near[1:]),
        mine,
        incoming,
    )
    came = [swapped(part, 2 * (i + 1)) for i, part in enumerate(sent)]
    scale = 1.0 / math.sqrt(total_tokens)
    done = small(
        functools.partial(join_kernel, scale), low, after(chip, in_next[0], in_this[0]), own, *came
    )
    others = [swapped(done, 2 * (i + 1)) for i in range(3)]
    half = jax.ShapeDtypeStruct((dim // 2, width), jnp.bfloat16)
    gathered = small(gather_kernel, half, after(chip, *in_next[1:], in_this[1]), done, *others)
    other_half = swapped(gathered, 1)
    weight_grad = small(
        widen_kernel, jax.ShapeDtypeStruct((dim, width), jnp.float32), core, gathered, other_half
    )
    return (input_grad, weight_grad)


def assemble(block_grid, far_rows):
    first_part = block_grid[:, :, 1]
    second_part = jnp.concatenate([block_grid[:, 1:, 0], far_rows[:, None]], axis=1)
    return jnp.concatenate([first_part, second_part], axis=2)


def window_grads(proj_win, delta_win, pos_bias, valid_count):
    scale_factor = 1.0 / math.sqrt(proj_win.shape[-1])
    queries = proj_win[:, :, :, 0]
    keys_part = proj_win[:, :, :, 1]
    values_part = proj_win[:, :, :, 2]
    scores = (
        jnp.einsum("nqhe,nkhe->nhqk", queries, keys_part, preferred_element_type=jnp.float32)
        * scale_factor
        + pos_bias[None]
    )
    positions = jnp.arange(proj_win.shape[1], dtype=jnp.int32)
    valid_keys = positions[None, :] < valid_count[:, None]
    scores = jnp.where(valid_keys[:, None, None, :], scores, -jnp.inf)
    row_max = jnp.max(scores, axis=-1, keepdims=True)
    weights = jnp.exp(scores - row_max)
    probs = weights / jnp.sum(weights, axis=-1, keepdims=True)
    grad_probs = jnp.einsum(
        "nqhe,nkhe->nhqk", delta_win, values_part, preferred_element_type=jnp.float32
    )
    grad_scores = probs * (grad_probs - jnp.sum(probs * grad_probs, axis=-1, keepdims=True))
    probs_low = probs.astype(jnp.bfloat16)
    grads_low = grad_scores.astype(jnp.bfloat16)
    grad_values = jnp.einsum(
        "nhqk,nqhe->nkhe", probs_low, delta_win, preferred_element_type=jnp.float32
    )
    grad_queries = (
        jnp.einsum("nhqk,nkhe->nqhe", grads_low, keys_part, preferred_element_type=jnp.float32)
        * scale_factor
    )
    grad_keys = (
        jnp.einsum("nhqk,nqhe->nkhe", grads_low, queries, preferred_element_type=jnp.float32)
        * scale_factor
    )
    return jnp.stack([grad_queries, grad_keys, grad_values], axis=3).astype(jnp.bfloat16)


def any_shards(activations, qkv_weight, attn_grad, pos_bias, key_counts):
    heads_here = pos_bias.shape[0]
    width_all = qkv_weight.shape[1]
    delta_width = attn_grad.shape[1]
    projected = jnp.dot(activations, qkv_weight, preferred_element_type=jnp.float32).astype(
        jnp.bfloat16
    )
    proj_grid = projected.reshape(WIN_ROWS, WIN_COLS, 2, HALF, width_all)
    delta_grid = attn_grad.reshape(WIN_ROWS, WIN_COLS, 2, HALF, delta_width)
    outgoing = jnp.concatenate([proj_grid[:, 0, 0], delta_grid[:, 0, 0]], axis=2)
    incoming = passed_along(outgoing, "lon", -1)
    proj_win = assemble(proj_grid, incoming[:, :, :width_all])
    delta_win = assemble(delta_grid, incoming[:, :, width_all:])
    gradients = window_grads(
        proj_win.reshape(WIN_ROWS * WIN_COLS, WIN, heads_here, 3, HEAD_DIM),
        delta_win.reshape(WIN_ROWS * WIN_COLS, WIN, heads_here, HEAD_DIM),
        pos_bias,
        key_counts,
    ).reshape(WIN_ROWS, WIN_COLS, WIN, width_all)
    leading = gradients[:, :, :HALF]
    trailing = gradients[:, :, HALF:]
    returned = passed_along(trailing[:, WIN_COLS - 1], "lon", 1)
    first_halves = jnp.concatenate([returned[:, None], trailing[:, : WIN_COLS - 1]], axis=1)
    grad_proj = jnp.stack([first_halves, leading], axis=2).reshape(BAND, width_all)
    local_grad = lax.dot_general(
        activations, grad_proj, (((0,), (0,)), ((), ())), preferred_element_type=jnp.float32
    )
    total_tokens = activations.shape[0] * lax.axis_size("lon")
    weight_grad = lax.psum(local_grad, "lon") / math.sqrt(total_tokens)
    partial_grad = lax.dot_general(
        grad_proj, qkv_weight, (((1,), (1,)), ((), ())), preferred_element_type=jnp.float32
    )
    partial_low = lax.optimization_barrier(partial_grad.astype(jnp.bfloat16)).astype(jnp.float32)
    input_grad = lax.psum_scatter(
        partial_low.astype(jnp.bfloat16), "head", scatter_dimension=0, tiled=True
    )
    return (input_grad, weight_grad)


def solution(mesh):
    placed = (P("lon", None), P(None, "head"), P("lon", "head"), P("head", None, None), P("lon"))
    on_line = mesh.shape["head"] == 4 and mesh.shape["lon"] == 8
    return jax.shard_map(
        line_shards if on_line else any_shards,
        mesh=mesh,
        in_specs=placed,
        out_specs=(P(("lon", "head"), None), P(None, "head")),
        check_vma=False,
    )
```

```python
import functools
import math

import jax
import jax.numpy as jnp
from jax import lax
from jax.experimental import pallas as pl
from jax.experimental.pallas import tpu as pltpu
from jax.sharding import PartitionSpec as P

HEAD_DIM = 64
WIN = 128
WIN_ROWS = 8
WIN_COLS = 2
HALF = WIN // 2
BAND = WIN_ROWS * WIN_COLS * WIN
ROW = WIN_COLS * WIN
VMEM_BYTES = 48 * 1024 * 1024
LARGE_VMEM_BYTES = 58 * 1024 * 1024
SMALL_VMEM_BYTES = 12 * 1024 * 1024

BESIDE, ACROSS = 1, 2
ORDER = (3, 1, 2, 0)
COST = pl.CostEstimate(flops=1_000_000, bytes_accessed=100_000, transcendentals=0)


def passed_along(shard, axis, by):
    size = lax.axis_size(axis)
    return lax.ppermute(shard, axis, [(i, (i + by) % size) for i in range(size)])


def swapped(shard, bits):
    size = lax.axis_size("lon")
    return lax.ppermute(shard, "lon", [(i, i ^ bits) for i in range(size)])


def attend(proj, delta, bias_ref, counts):
    scale = 1.0 / math.sqrt(HEAD_DIM)
    low = lax.broadcasted_iota(jnp.int32, (WIN, 2 * HEAD_DIM), 1) < HEAD_DIM
    key_at = lax.broadcasted_iota(jnp.int32, (WIN, WIN), 0)

    def both(pair):
        zero = jnp.zeros_like(pair)
        return jnp.concatenate([jnp.where(low, pair, zero), jnp.where(low, zero, pair)], axis=0)

    def rolled(x):
        return pltpu.roll(x, HEAD_DIM, 1)

    def dot(x, y, on):
        return lax.dot_general(x, y, (on, ((), ())), preferred_element_type=jnp.float32)

    pairs = proj.shape[1] // (6 * HEAD_DIM)
    units = [(w, p) for w in range(2) for p in range(pairs)]
    scored, softened, tiles = [], [], []
    for w, p in units:
        rows = slice(w * WIN, (w + 1) * WIN)
        at = [proj[rows, (3 * p + i) * WIN : (3 * p + i + 1) * WIN] for i in range(3)]
        queries = jnp.where(low, at[0], at[1]).astype(jnp.bfloat16)
        keys = rolled(jnp.where(low, at[2], at[0])).astype(jnp.bfloat16)
        values = jnp.where(low, at[1], at[2]).astype(jnp.bfloat16)
        grads = delta[rows, p * WIN : (p + 1) * WIN]
        two_keys = both(keys)
        scores = dot(two_keys, queries, ((1,), (1,)))
        grad_probs = dot(both(values), grads, ((1,), (1,)))
        scored.append((queries, two_keys, grads, scores, grad_probs))
    for (w, p), (queries, two_keys, grads, scores, grad_probs) in zip(units, scored):
        probs_low, grads_low = [], []
        for h in range(2):
            head = slice(h * WIN, (h + 1) * WIN)
            biased = scores[head] * scale + bias_ref[2 * p + h]
            biased = jnp.where(key_at < counts[w], biased, -jnp.inf)
            weights = jnp.exp(biased - jnp.max(biased, axis=0, keepdims=True))
            probs = weights * (1.0 / jnp.sum(weights, axis=0, keepdims=True))
            inner = jnp.sum(probs * grad_probs[head], axis=0, keepdims=True)
            probs_low.append(probs.astype(jnp.bfloat16))
            grads_low.append((probs * (grad_probs[head] - inner)).astype(jnp.bfloat16))
        softened.append((queries, two_keys, grads, probs_low, grads_low))
    for queries, two_keys, grads, probs_low, grads_low in softened:
        grad_values = dot(jnp.concatenate(probs_low, axis=1), both(grads), ((1,), (0,)))
        grad_keys = dot(jnp.concatenate(grads_low, axis=1), both(queries), ((1,), (0,)))
        grad_queries = dot(jnp.concatenate(grads_low, axis=0), two_keys, ((0,), (0,))) * scale
        grad_keys = rolled(grad_keys * scale)
        tiles.append(
            [
                jnp.where(low, grad_queries, grad_keys).astype(jnp.bfloat16),
                jnp.where(low, grad_values, grad_queries).astype(jnp.bfloat16),
                jnp.where(low, grad_keys, grad_values).astype(jnp.bfloat16),
            ]
        )
    return jnp.concatenate(
        [jnp.concatenate(sum(tiles[w * pairs : (w + 1) * pairs], []), axis=1) for w in range(2)],
        axis=0,
    )


def block_at(head, step):
    bits = jnp.where(step == 3, ORDER[3], ORDER[2])
    bits = jnp.where(step == 1, ORDER[1], bits)
    return head ^ jnp.where(step == 0, ORDER[0], bits)


def pack_kernel(act_ref, delta_ref, out_ref, sems):
    dim = act_ref.shape[2]
    copies = [
        pltpu.make_async_copy(
            act_ref.at[:, pl.ds(0, HALF), :], out_ref.at[:, :, pl.ds(0, dim)], sems.at[0]
        ),
        pltpu.make_async_copy(
            delta_ref.at[:, pl.ds(0, HALF), :],
            out_ref.at[:, :, pl.ds(dim, delta_ref.shape[2])],
            sems.at[1],
        ),
    ]
    for copy in copies:
        copy.start()
    for copy in copies:
        copy.wait()


def first_rows(act, delta):
    dim, delta_width = act.shape[1], delta.shape[1]
    anywhere = pl.BlockSpec(memory_space=pl.ANY)
    return pl.pallas_call(
        pack_kernel,
        in_specs=[anywhere, anywhere],
        out_specs=pl.BlockSpec(memory_space=pltpu.VMEM),
        out_shape=jax.ShapeDtypeStruct((WIN_ROWS, HALF, dim + delta_width), act.dtype),
        scratch_shapes=[pltpu.SemaphoreType.DMA((2,))],
        name="first_rows",
    )(act.reshape(WIN_ROWS, ROW, dim), delta.reshape(WIN_ROWS, ROW, delta_width))


def turned_biases(bias_ref, turned_ref):
    @pl.when(pl.program_id(0) == 0)
    def _():
        for h in range(bias_ref.shape[0]):
            turned_ref[h] = bias_ref[h].T


def counts_of(counts_ref, block, column):
    first = block * 2 * WIN_COLS + column
    return [counts_ref[first], counts_ref[first + WIN_COLS]]


def part_of(grads, weight):
    return lax.dot_general(
        grads, weight, (((1,), (1,)), ((), ())), preferred_element_type=jnp.float32
    ).astype(jnp.bfloat16)


def near_kernel(
    start, steps, head_ref, counts_ref, act_ref, delta_ref, weight_ref, bias_ref, *rest
):
    *outs, held_ref = rest[-5 - steps : -4]
    turned_ref, parts_ref, grads_ref, sems = rest[-4:]
    turned_biases(bias_ref, turned_ref)
    at = [slice(i * ROW + HALF, i * ROW + HALF + WIN) for i in range(2)]
    rows = jnp.concatenate([act_ref[s, :] for s in at], axis=0)
    delta = jnp.concatenate([delta_ref[s, :] for s in at], axis=0)
    weight = weight_ref[...]
    proj = jnp.dot(rows, weight, preferred_element_type=jnp.float32)
    step = pl.program_id(0)
    counts = counts_of(counts_ref, block_at(head_ref[0], step + start), 0)
    grads = attend(proj, delta, turned_ref, counts)
    grads_ref[step] = grads
    parts_ref[step] = part_of(grads, weight)
    tokens = 2 * WIN
    copies = [
        [
            pltpu.make_async_copy(parts_ref.at[i], outs[i], sems.at[0, i]),
            pltpu.make_async_copy(
                grads_ref.at[i], held_ref.at[pl.ds((start + i) * tokens, tokens), :], sems.at[1, i]
            ),
        ]
        for i in range(steps)
    ]
    for i in range(steps):

        @pl.when(step == i)
        def _():
            for copy in copies[i]:
                copy.start()

    @pl.when(step == steps - 1)
    def _():
        for copy in sum(copies, []):
            copy.wait()


def near_windows(start, steps, head, counts, act, delta, weight, bias, held):
    width, dim, delta_width = weight.shape[1], act.shape[1], delta.shape[1]
    blocked = lambda j, head_ref, counts_ref: (block_at(head_ref[0], j + start), 0)
    whole2 = lambda j, head_ref, counts_ref: (0, 0)
    whole3 = lambda j, head_ref, counts_ref: (0, 0, 0)
    tokens = 2 * WIN
    operands = [act, delta, weight, bias]
    specs = [
        pl.BlockSpec((2 * ROW, dim), blocked),
        pl.BlockSpec((2 * ROW, delta_width), blocked),
        pl.BlockSpec(weight.shape, whole2),
        pl.BlockSpec(bias.shape, whole3),
    ]
    aliases = {}
    if held is not None:
        aliases = {2 + len(operands): steps}
        operands.append(held)
        specs.append(pl.BlockSpec(memory_space=pl.ANY))
    part = jax.ShapeDtypeStruct((tokens, dim), jnp.bfloat16)
    return pl.pallas_call(
        functools.partial(near_kernel, start, steps),
        grid_spec=pltpu.PrefetchScalarGridSpec(
            num_scalar_prefetch=2,
            grid=(steps,),
            in_specs=specs,
            out_specs=[pl.BlockSpec(memory_space=pl.ANY)] * (steps + 1),
            scratch_shapes=[
                pltpu.VMEM(bias.shape, bias.dtype),
                pltpu.VMEM((steps, tokens, dim), jnp.bfloat16),
                pltpu.VMEM((steps, tokens, width), jnp.bfloat16),
                pltpu.SemaphoreType.DMA((2, steps)),
            ],
        ),
        out_shape=[part] * steps + [jax.ShapeDtypeStruct((4 * tokens, width), jnp.bfloat16)],
        input_output_aliases=aliases,
        compiler_params=pltpu.CompilerParams(vmem_limit_bytes=VMEM_BYTES if start == 0 else LARGE_VMEM_BYTES),
        cost_estimate=COST,
        name="near_windows",
    )(head, counts, *operands)


def far_kernel(
    head_ref, core_ref, counts_ref, act_ref, delta_ref, far_ref, weight_ref, bias_ref, held_ref, *rest
):
    outs, send_ref, keep_ref, turned_ref, total_ref, parts_ref, sems = rest[:7], *rest[7:]
    turned_biases(bias_ref, turned_ref)
    dim, delta_width = act_ref.shape[1], delta_ref.shape[1]
    step = pl.program_id(0)

    def mixed(near_ref, low, high):
        pieces = []
        for i in range(2):
            pieces.append(near_ref[(i + 1) * ROW - HALF : (i + 1) * ROW, :])
            pieces.append(far_ref[i * HALF : (i + 1) * HALF, low:high])
        return jnp.concatenate(pieces, axis=0)

    rows = mixed(act_ref, 0, dim)
    delta = mixed(delta_ref, dim, dim + delta_width)
    weight = weight_ref[...]
    proj = jnp.dot(rows, weight, preferred_element_type=jnp.float32)
    counts = counts_of(counts_ref, block_at(head_ref[0], step), 1)
    grads = attend(proj, delta, turned_ref, counts)
    part = part_of(grads, weight)
    parts_ref[step, :HALF] = part[HALF:WIN]
    parts_ref[step, HALF:WIN] = part[WIN + HALF :]
    parts_ref[step, WIN : WIN + HALF] = part[:HALF]
    parts_ref[step, WIN + HALF :] = part[WIN : WIN + HALF]
    halves = [pl.ds(0, WIN), pl.ds(WIN, WIN)]
    copies = [[pltpu.make_async_copy(parts_ref.at[0], outs[0], sems.at[0, 0])]]
    copies += [
        [
            pltpu.make_async_copy(parts_ref.at[i, halves[j], :], outs[2 * i - 1 + j], sems.at[i, j])
            for j in range(2)
        ]
        for i in range(1, 4)
    ]
    for i in range(4):

        @pl.when(step == i)
        def _():
            for copy in copies[i]:
                copy.start()

    near_rows = [act_ref[i * ROW + HALF : i * ROW + HALF + WIN, :] for i in range(2)]
    all_rows = jnp.concatenate(near_rows + [rows], axis=0)
    all_grads = jnp.concatenate([held_ref[...], grads], axis=0)
    @pl.when(step == 0)
    def _():
        total_ref[...] = jnp.zeros_like(total_ref)

    total_ref[...] += lax.dot_general(
        all_rows, all_grads, (((0,), (0,)), ((), ())), preferred_element_type=jnp.float32
    )

    @pl.when(step == 3)
    def _():
        half = dim // 2
        core = core_ref[0]
        keep_ref[...] = total_ref[pl.ds(pl.multiple_of(core * half, half), half), :]
        send_ref[...] = total_ref[pl.ds(pl.multiple_of((1 - core) * half, half), half), :].astype(
            jnp.bfloat16
        )
        for copy in sum(copies, []):
            copy.wait()


def far_windows(head, core, counts, act, delta, far, weight, bias, held):
    width, dim, delta_width = weight.shape[1], act.shape[1], delta.shape[1]
    blocked = lambda j, head_ref, core_ref, counts_ref: (block_at(head_ref[0], j), 0)
    whole2 = lambda j, head_ref, core_ref, counts_ref: (0, 0)
    whole3 = lambda j, head_ref, core_ref, counts_ref: (0, 0, 0)
    parts = [
        jax.ShapeDtypeStruct((tokens, dim), jnp.bfloat16)
        for tokens in (2 * WIN, WIN, WIN, WIN, WIN, WIN, WIN)
    ]
    return pl.pallas_call(
        far_kernel,
        grid_spec=pltpu.PrefetchScalarGridSpec(
            num_scalar_prefetch=3,
            grid=(4,),
            in_specs=[
                pl.BlockSpec((2 * ROW, dim), blocked),
                pl.BlockSpec((2 * ROW, delta_width), blocked),
                pl.BlockSpec((WIN, dim + delta_width), blocked),
                pl.BlockSpec(weight.shape, whole2),
                pl.BlockSpec(bias.shape, whole3),
                pl.BlockSpec((2 * WIN, width), lambda j, head_ref, core_ref, counts_ref: (j, 0)),
            ],
            out_specs=[pl.BlockSpec(memory_space=pl.ANY)] * 7
            + [pl.BlockSpec((dim // 2, width), whole2)] * 2,
            scratch_shapes=[
                pltpu.VMEM(bias.shape, bias.dtype),
                pltpu.VMEM((dim, width), jnp.float32),
                pltpu.VMEM((4, 2 * WIN, dim), jnp.bfloat16),
                pltpu.SemaphoreType.DMA((4, 2)),
            ],
        ),
        out_shape=parts
        + [jax.ShapeDtypeStruct((dim // 2, width), dtype) for dtype in (jnp.bfloat16, jnp.float32)],
        compiler_params=pltpu.CompilerParams(vmem_limit_bytes=LARGE_VMEM_BYTES),
        cost_estimate=COST,
        name="far_windows",
    )(head, core, counts, act, delta, far, weight, bias, held)


def split_kernel(chip_ref, mine_ref, theirs_ref, own_ref, *outs):
    rows = own_ref.shape[0]
    for bits in range(4):
        at = pl.ds(pl.multiple_of((chip_ref[0] ^ bits) * rows, rows), rows)
        total = mine_ref[at, :] + theirs_ref[at, :].astype(jnp.float32)
        if bits:
            outs[bits - 1][...] = total.astype(jnp.bfloat16)
        else:
            own_ref[...] = total


def join_kernel(scale, chip_ref, own_ref, a_ref, b_ref, c_ref, out_ref):
    total = own_ref[...] + a_ref[...].astype(jnp.float32)
    total = (total + b_ref[...].astype(jnp.float32)) + c_ref[...].astype(jnp.float32)
    out_ref[...] = (total * scale).astype(jnp.bfloat16)


def gather_kernel(chip_ref, own_ref, a_ref, b_ref, c_ref, out_ref):
    rows = own_ref.shape[0]
    for bits, ref in enumerate((own_ref, a_ref, b_ref, c_ref)):
        out_ref[pl.ds(pl.multiple_of((chip_ref[0] ^ bits) * rows, rows), rows), :] = ref[...]


def widen_kernel(core_ref, mine_ref, theirs_ref, out_ref):
    rows = mine_ref.shape[0]
    for other, ref in enumerate((mine_ref, theirs_ref)):
        at = pl.ds(pl.multiple_of((core_ref[0] ^ other) * rows, rows), rows)
        out_ref[at, :] = ref[...].astype(jnp.float32)


def small(kernel, out_shape, place, *operands):
    vmem = pl.BlockSpec(memory_space=pltpu.VMEM)
    several = isinstance(out_shape, list)
    return pl.pallas_call(
        kernel,
        in_specs=[pl.BlockSpec(memory_space=pltpu.SMEM)] + [vmem] * len(operands),
        out_specs=[vmem] * len(out_shape) if several else vmem,
        out_shape=out_shape,
        compiler_params=pltpu.CompilerParams(vmem_limit_bytes=SMALL_VMEM_BYTES),
        cost_estimate=COST,
    )(place, *operands)


def after(x, *others):
    return lax.optimization_barrier((x, *others))[0]


def add(*parts):
    total = parts[0].astype(jnp.float32)
    for part in parts[1:]:
        total = total + part.astype(jnp.float32)
    return total.astype(jnp.bfloat16)


def line_shards(activations, qkv_weight, attn_grad, pos_bias, key_counts):
    dim, width = qkv_weight.shape
    total_tokens = activations.shape[0] * lax.axis_size("lon")
    head = lax.axis_index("head").reshape(1)
    lon = lax.axis_index("lon")
    core, chip = (lon % 2).reshape(1), (lon // 2).reshape(1)

    def hop(x, bits):
        return lax.ppermute(x, "head", [(i, i ^ bits) for i in range(lax.axis_size("head"))])

    far = passed_along(first_rows(activations, attn_grad), "lon", -1)
    here = (activations, attn_grad, qkv_weight, pos_bias)
    first, held = near_windows(0, 1, head, key_counts, *here, None)
    in_near = [hop(first, BESIDE)]
    *near, held = near_windows(1, 3, head, key_counts, *here, held)
    in_near.append(hop(near[0], BESIDE))
    in_near.append(hop(after(add(near[1], in_near[0]), far), ACROSS))
    far = far.reshape(WIN_ROWS * HALF, far.shape[2])
    *parts, outgoing, mine = far_windows(
        head, core, key_counts, activations, attn_grad, far, qkv_weight, pos_bias, held
    )
    incoming = swapped(outgoing, 1)
    both_a, next_b, this_b, next_c, this_c, next_d, this_d = parts
    in_both, more_next = hop(both_a, BESIDE), hop(next_b, BESIDE)
    near_sum = add(near[2], *in_near[1:])

    block = (dim // 8, width)
    low = jax.ShapeDtypeStruct(block, jnp.bfloat16)
    own, *sent = small(
        split_kernel,
        [jax.ShapeDtypeStruct(block, jnp.float32), low, low, low],
        after(chip, near_sum),
        mine,
        incoming,
    )
    came = [swapped(part, 2 * (i + 1)) for i, part in enumerate(sent)]

    in_both = after(in_both, own, *came)
    out_next, out_this = add(next_c, in_both[:WIN]), add(this_c, in_both[WIN:])
    more_this = hop(after(this_b, out_next), BESIDE)
    over_next, over_this = hop(out_next, ACROSS), hop(out_this, ACROSS)

    scale = 1.0 / math.sqrt(total_tokens)
    done = small(functools.partial(join_kernel, scale), low, after(chip, out_this), own, *came)
    others = [swapped(done, 2 * (i + 1)) for i in range(3)]

    next_sum = add(next_d, more_next, over_next)
    back = passed_along(next_sum, "lon", 1)
    half = jax.ShapeDtypeStruct((dim // 2, width), jnp.bfloat16)
    gathered = small(gather_kernel, half, chip, done, *others)
    other_half = swapped(gathered, 1)
    weight_grad = small(
        widen_kernel, jax.ShapeDtypeStruct((dim, width), jnp.float32), core, gathered, other_half
    )
    this_sum = add(this_d, more_this, over_this)
    input_grad = jnp.concatenate(
        [x.reshape(2, -1, dim) for x in (back, near_sum, this_sum)], axis=1
    ).reshape(2 * ROW, dim)

    return (input_grad, weight_grad)


def assemble(block_grid, far_rows):
    first_part = block_grid[:, :, 1]
    second_part = jnp.concatenate([block_grid[:, 1:, 0], far_rows[:, None]], axis=1)
    return jnp.concatenate([first_part, second_part], axis=2)


def window_grads(proj_win, delta_win, pos_bias, valid_count):
    scale_factor = 1.0 / math.sqrt(proj_win.shape[-1])
    queries = proj_win[:, :, :, 0]
    keys_part = proj_win[:, :, :, 1]
    values_part = proj_win[:, :, :, 2]
    scores = (
        jnp.einsum("nqhe,nkhe->nhqk", queries, keys_part, preferred_element_type=jnp.float32)
        * scale_factor
        + pos_bias[None]
    )
    positions = jnp.arange(proj_win.shape[1], dtype=jnp.int32)
    valid_keys = positions[None, :] < valid_count[:, None]
    scores = jnp.where(valid_keys[:, None, None, :], scores, -jnp.inf)
    row_max = jnp.max(scores, axis=-1, keepdims=True)
    weights = jnp.exp(scores - row_max)
    probs = weights / jnp.sum(weights, axis=-1, keepdims=True)
    grad_probs = jnp.einsum(
        "nqhe,nkhe->nhqk", delta_win, values_part, preferred_element_type=jnp.float32
    )
    grad_scores = probs * (grad_probs - jnp.sum(probs * grad_probs, axis=-1, keepdims=True))
    probs_low = probs.astype(jnp.bfloat16)
    grads_low = grad_scores.astype(jnp.bfloat16)
    grad_values = jnp.einsum(
        "nhqk,nqhe->nkhe", probs_low, delta_win, preferred_element_type=jnp.float32
    )
    grad_queries = (
        jnp.einsum("nhqk,nkhe->nqhe", grads_low, keys_part, preferred_element_type=jnp.float32)
        * scale_factor
    )
    grad_keys = (
        jnp.einsum("nhqk,nqhe->nkhe", grads_low, queries, preferred_element_type=jnp.float32)
        * scale_factor
    )
    return jnp.stack([grad_queries, grad_keys, grad_values], axis=3).astype(jnp.bfloat16)


def any_shards(activations, qkv_weight, attn_grad, pos_bias, key_counts):
    heads_here = pos_bias.shape[0]
    width_all = qkv_weight.shape[1]
    delta_width = attn_grad.shape[1]
    projected = jnp.dot(activations, qkv_weight, preferred_element_type=jnp.float32).astype(
        jnp.bfloat16
    )
    proj_grid = projected.reshape(WIN_ROWS, WIN_COLS, 2, HALF, width_all)
    delta_grid = attn_grad.reshape(WIN_ROWS, WIN_COLS, 2, HALF, delta_width)
    outgoing = jnp.concatenate([proj_grid[:, 0, 0], delta_grid[:, 0, 0]], axis=2)
    incoming = passed_along(outgoing, "lon", -1)
    proj_win = assemble(proj_grid, incoming[:, :, :width_all])
    delta_win = assemble(delta_grid, incoming[:, :, width_all:])
    gradients = window_grads(
        proj_win.reshape(WIN_ROWS * WIN_COLS, WIN, heads_here, 3, HEAD_DIM),
        delta_win.reshape(WIN_ROWS * WIN_COLS, WIN, heads_here, HEAD_DIM),
        pos_bias,
        key_counts,
    ).reshape(WIN_ROWS, WIN_COLS, WIN, width_all)
    leading = gradients[:, :, :HALF]
    trailing = gradients[:, :, HALF:]
    returned = passed_along(trailing[:, WIN_COLS - 1], "lon", 1)
    first_halves = jnp.concatenate([returned[:, None], trailing[:, : WIN_COLS - 1]], axis=1)
    grad_proj = jnp.stack([first_halves, leading], axis=2).reshape(BAND, width_all)
    local_grad = lax.dot_general(
        activations, grad_proj, (((0,), (0,)), ((), ())), preferred_element_type=jnp.float32
    )
    total_tokens = activations.shape[0] * lax.axis_size("lon")
    weight_grad = lax.psum(local_grad, "lon") / math.sqrt(total_tokens)
    partial_grad = lax.dot_general(
        grad_proj, qkv_weight, (((1,), (1,)), ((), ())), preferred_element_type=jnp.float32
    )
    partial_low = lax.optimization_barrier(partial_grad.astype(jnp.bfloat16)).astype(jnp.float32)
    input_grad = lax.psum_scatter(
        partial_low.astype(jnp.bfloat16), "head", scatter_dimension=0, tiled=True
    )
    return (input_grad, weight_grad)


def solution(mesh):
    placed = (P("lon", None), P(None, "head"), P("lon", "head"), P("head", None, None), P("lon"))
    on_line = mesh.shape["head"] == 4 and mesh.shape["lon"] == 8
    return jax.shard_map(
        line_shards if on_line else any_shards,
        mesh=mesh,
        in_specs=placed,
        out_specs=(P(("lon", "head"), None), P(None, "head")),
        check_vma=False,
    )
```

```python
import functools
import math

import jax
import jax.numpy as jnp
from jax import lax
from jax.experimental import pallas as pl
from jax.experimental.pallas import tpu as pltpu
from jax.sharding import PartitionSpec as P

HEAD_DIM = 64
WIN = 128
WIN_ROWS = 8
WIN_COLS = 2
HALF = WIN // 2
BAND = WIN_ROWS * WIN_COLS * WIN
ROW = WIN_COLS * WIN
NEAR_VMEM_BYTES = 48 * 1024 * 1024
LARGE_VMEM_BYTES = 56 * 1024 * 1024
HELD_ROWS = 12 * 1024
SMALL_VMEM_BYTES = 12 * 1024 * 1024

BESIDE, ACROSS = 1, 2
ORDER = (3, 1, 2, 0)
COST = pl.CostEstimate(flops=1_000_000, bytes_accessed=100_000, transcendentals=0)


def passed_along(shard, axis, by):
    size = lax.axis_size(axis)
    return lax.ppermute(shard, axis, [(i, (i + by) % size) for i in range(size)])


def swapped(shard, bits):
    size = lax.axis_size("lon")
    return lax.ppermute(shard, "lon", [(i, i ^ bits) for i in range(size)])


def attend(proj, delta, bias_ref, counts):
    scale = 1.0 / math.sqrt(HEAD_DIM)
    low = lax.broadcasted_iota(jnp.int32, (WIN, 2 * HEAD_DIM), 1) < HEAD_DIM
    key_at = lax.broadcasted_iota(jnp.int32, (WIN, WIN), 0)

    def both(pair):
        zero = jnp.zeros_like(pair)
        return jnp.concatenate([jnp.where(low, pair, zero), jnp.where(low, zero, pair)], axis=0)

    def rolled(x):
        return pltpu.roll(x, HEAD_DIM, 1)

    def dot(x, y, on):
        return lax.dot_general(x, y, (on, ((), ())), preferred_element_type=jnp.float32)

    pairs = proj.shape[1] // (6 * HEAD_DIM)
    units = [(w, p) for w in range(2) for p in range(pairs)]
    scored, softened, tiles = [], [], []
    for w, p in units:
        rows = slice(w * WIN, (w + 1) * WIN)
        at = [proj[rows, (3 * p + i) * WIN : (3 * p + i + 1) * WIN] for i in range(3)]
        queries = jnp.where(low, at[0], at[1]).astype(jnp.bfloat16)
        keys = rolled(jnp.where(low, at[2], at[0])).astype(jnp.bfloat16)
        values = jnp.where(low, at[1], at[2]).astype(jnp.bfloat16)
        grads = delta[rows, p * WIN : (p + 1) * WIN]
        two_keys = both(keys)
        scores = dot(two_keys, queries, ((1,), (1,)))
        grad_probs = dot(both(values), grads, ((1,), (1,)))
        scored.append((queries, two_keys, grads, scores, grad_probs))
    for (w, p), (queries, two_keys, grads, scores, grad_probs) in zip(units, scored):
        probs_low, grads_low = [], []
        for h in range(2):
            head = slice(h * WIN, (h + 1) * WIN)
            biased = scores[head] * scale + bias_ref[2 * p + h]
            biased = jnp.where(key_at < counts[w], biased, -jnp.inf)
            weights = jnp.exp(biased - jnp.max(biased, axis=0, keepdims=True))
            probs = weights * (1.0 / jnp.sum(weights, axis=0, keepdims=True))
            inner = jnp.sum(probs * grad_probs[head], axis=0, keepdims=True)
            probs_low.append(probs.astype(jnp.bfloat16))
            grads_low.append((probs * (grad_probs[head] - inner)).astype(jnp.bfloat16))
        softened.append((queries, two_keys, grads, probs_low, grads_low))
    for queries, two_keys, grads, probs_low, grads_low in softened:
        grad_values = dot(jnp.concatenate(probs_low, axis=1), both(grads), ((1,), (0,)))
        grad_keys = dot(jnp.concatenate(grads_low, axis=1), both(queries), ((1,), (0,)))
        grad_queries = dot(jnp.concatenate(grads_low, axis=0), two_keys, ((0,), (0,))) * scale
        grad_keys = rolled(grad_keys * scale)
        tiles.append(
            [
                jnp.where(low, grad_queries, grad_keys).astype(jnp.bfloat16),
                jnp.where(low, grad_values, grad_queries).astype(jnp.bfloat16),
                jnp.where(low, grad_keys, grad_values).astype(jnp.bfloat16),
            ]
        )
    return jnp.concatenate(
        [jnp.concatenate(sum(tiles[w * pairs : (w + 1) * pairs], []), axis=1) for w in range(2)],
        axis=0,
    )


def block_at(head, step):
    bits = jnp.where(step == 3, ORDER[3], ORDER[2])
    bits = jnp.where(step == 1, ORDER[1], bits)
    return head ^ jnp.where(step == 0, ORDER[0], bits)


def pack_kernel(act_ref, delta_ref, out_ref, sems):
    dim = act_ref.shape[2]
    copies = [
        pltpu.make_async_copy(
            act_ref.at[:, pl.ds(0, HALF), :], out_ref.at[:, :, pl.ds(0, dim)], sems.at[0]
        ),
        pltpu.make_async_copy(
            delta_ref.at[:, pl.ds(0, HALF), :],
            out_ref.at[:, :, pl.ds(dim, delta_ref.shape[2])],
            sems.at[1],
        ),
    ]
    for copy in copies:
        copy.start()
    for copy in copies:
        copy.wait()


def first_rows(act, delta):
    dim, delta_width = act.shape[1], delta.shape[1]
    anywhere = pl.BlockSpec(memory_space=pl.ANY)
    return pl.pallas_call(
        pack_kernel,
        in_specs=[anywhere, anywhere],
        out_specs=pl.BlockSpec(memory_space=pltpu.VMEM),
        out_shape=jax.ShapeDtypeStruct((WIN_ROWS, HALF, dim + delta_width), act.dtype),
        scratch_shapes=[pltpu.SemaphoreType.DMA((2,))],
        name="first_rows",
    )(act.reshape(WIN_ROWS, ROW, dim), delta.reshape(WIN_ROWS, ROW, delta_width))


def turned_biases(bias_ref, turned_ref):
    for h in range(bias_ref.shape[0]):
        turned_ref[h] = bias_ref[h].T


def counts_of(counts_ref, block, column):
    first = block * 2 * WIN_COLS + column
    return [counts_ref[first], counts_ref[first + WIN_COLS]]


def part_of(grads, weight):
    return lax.dot_general(
        grads, weight, (((1,), (1,)), ((), ())), preferred_element_type=jnp.float32
    ).astype(jnp.bfloat16)


def near_kernel(start, steps, head_ref, counts_ref, weight_ref, bias_ref, delta_ref, act_ref, *rest):
    *outs, held_ref = rest[-6 - steps : -5]
    turned_ref, rows_ref, parts_ref, grads_ref, sems = rest[-5:]
    tokens = 2 * WIN

    def fetch(k):
        block = block_at(head_ref[0], start + k)
        return pltpu.make_async_copy(
            act_ref.at[pl.ds(2 * block, 2), pl.ds(HALF, WIN), :], rows_ref.at[k], sems.at[2, k]
        )

    def put(k):
        held_rows = held_ref.at[pl.ds((start + k) * tokens, tokens), :]
        return [
            pltpu.make_async_copy(parts_ref.at[k], outs[k], sems.at[0, k]),
            pltpu.make_async_copy(grads_ref.at[k], held_rows, sems.at[1, k]),
        ]

    fetch(0).start()
    turned_biases(bias_ref, turned_ref)
    for k in range(steps):
        block = block_at(head_ref[0], start + k)
        base = pl.multiple_of(block * 2 * ROW, 2 * ROW)
        delta = [delta_ref[pl.ds(base + i * ROW + HALF, WIN), :] for i in range(2)]
        fetch(k).wait()
        if k + 1 < steps:
            fetch(k + 1).start()
        weight = weight_ref[...]
        rows = rows_ref[k].reshape(tokens, weight.shape[0])
        proj = jnp.dot(rows, weight, preferred_element_type=jnp.float32)
        counts = counts_of(counts_ref, block, 0)
        grads = attend(proj, jnp.concatenate(delta, axis=0), turned_ref, counts)
        grads_ref[k] = grads
        parts_ref[k] = part_of(grads, weight)
        for copy in put(k):
            copy.start()
    for k in range(steps):
        for copy in put(k):
            copy.wait()


VMEM = pl.BlockSpec(memory_space=pltpu.VMEM)
SMEM = pl.BlockSpec(memory_space=pltpu.SMEM)
ANYWHERE = pl.BlockSpec(memory_space=pl.ANY)


def near_windows(start, steps, head, counts, act, delta, weight, bias, held):
    width, dim = weight.shape[1], act.shape[1]
    tokens = 2 * WIN
    operands = [head, counts, weight, bias, delta, act.reshape(WIN_ROWS, ROW, dim)]
    specs = [SMEM, SMEM, VMEM, VMEM, VMEM, ANYWHERE]
    aliases = {}
    if held is not None:
        aliases = {len(operands): steps}
        operands.append(held)
        specs.append(ANYWHERE)
    part = jax.ShapeDtypeStruct((tokens, dim), jnp.bfloat16)
    return pl.pallas_call(
        functools.partial(near_kernel, start, steps),
        in_specs=specs,
        out_specs=[ANYWHERE] * (steps + 1),
        scratch_shapes=[
            pltpu.VMEM(bias.shape, bias.dtype),
            pltpu.VMEM((steps, 2, WIN, dim), jnp.bfloat16),
            pltpu.VMEM((steps, tokens, dim), jnp.bfloat16),
            pltpu.VMEM((steps, tokens, width), jnp.bfloat16),
            pltpu.SemaphoreType.DMA((3, steps)),
        ],
        out_shape=[part] * steps + [jax.ShapeDtypeStruct((HELD_ROWS, width), jnp.bfloat16)],
        input_output_aliases=aliases,
        compiler_params=pltpu.CompilerParams(vmem_limit_bytes=NEAR_VMEM_BYTES),
        cost_estimate=COST,
        name="near_windows",
    )(*operands)


def far_kernel(
    head_ref, core_ref, counts_ref, weight_ref, bias_ref, delta_ref, act_ref, far_ref, held_ref, *rest
):
    outs, send_ref, keep_ref, *scratch = rest[:7], *rest[7:]
    turned_ref, total_ref, rows_ref, grads_ref, halo_ref, parts_ref, in_sems, out_sems = scratch
    dim, delta_width = act_ref.shape[2], delta_ref.shape[1]

    def fetch(k):
        block = block_at(head_ref[0], k)
        copies = [
            (
                act_ref.at[pl.ds(2 * block, 2), pl.ds(HALF, ROW - HALF), :],
                rows_ref.at[k, :, pl.ds(0, ROW - HALF), :],
            ),
            (
                far_ref.at[pl.ds(2 * block, 2), :, pl.ds(0, dim)],
                rows_ref.at[k, :, pl.ds(ROW - HALF, HALF), :],
            ),
            (far_ref.at[pl.ds(2 * block, 2), :, pl.ds(dim, delta_width)], halo_ref.at[k]),
            (held_ref.at[pl.ds(2 * k, 2), :, :], grads_ref.at[k, :, pl.ds(0, WIN), :]),
        ]
        return [
            pltpu.make_async_copy(source, target, in_sems.at[k, i])
            for i, (source, target) in enumerate(copies)
        ]

    halves = [pl.ds(0, WIN), pl.ds(WIN, WIN)]
    put = [[pltpu.make_async_copy(parts_ref.at[0], outs[0], out_sems.at[0, 0])]]
    put += [
        [
            pltpu.make_async_copy(parts_ref.at[k, halves[j], :], outs[2 * k - 1 + j], out_sems.at[k, j])
            for j in range(2)
        ]
        for k in range(1, 4)
    ]
    for copy in fetch(0):
        copy.start()
    turned_biases(bias_ref, turned_ref)
    for k in range(4):
        block = block_at(head_ref[0], k)
        base = pl.multiple_of(block * 2 * ROW, 2 * ROW)
        for copy in fetch(k):
            copy.wait()
        if k < 3:
            for copy in fetch(k + 1):
                copy.start()
        delta = []
        for i in range(2):
            delta += [delta_ref[pl.ds(base + (i + 1) * ROW - HALF, HALF), :], halo_ref[k, i]]
        weight = weight_ref[...]
        rows = rows_ref[k, :, WIN:, :].reshape(2 * WIN, dim)
        proj = jnp.dot(rows, weight, preferred_element_type=jnp.float32)
        counts = counts_of(counts_ref, block, 1)
        grads = attend(proj, jnp.concatenate(delta, axis=0), turned_ref, counts)
        grads_ref[k, 0, WIN:, :] = grads[:WIN]
        grads_ref[k, 1, WIN:, :] = grads[WIN:]
        part = part_of(grads, weight)
        parts_ref[k, :HALF] = part[HALF:WIN]
        parts_ref[k, HALF:WIN] = part[WIN + HALF :]
        parts_ref[k, WIN : WIN + HALF] = part[:HALF]
        parts_ref[k, WIN + HALF :] = part[WIN : WIN + HALF]
        for copy in put[k]:
            copy.start()
        product = lax.dot_general(
            rows_ref[k].reshape(2 * ROW, dim),
            grads_ref[k].reshape(2 * ROW, weight.shape[1]),
            (((0,), (0,)), ((), ())),
            preferred_element_type=jnp.float32,
        )
        if k:
            total_ref[...] += product
        else:
            total_ref[...] = product
    half = dim // 2
    core = core_ref[0]
    send_ref[...] = total_ref[pl.ds(pl.multiple_of((1 - core) * half, half), half), :].astype(
        jnp.bfloat16
    )
    keep_ref[...] = total_ref[pl.ds(pl.multiple_of(core * half, half), half), :]
    for copy in sum(put, []):
        copy.wait()


def far_windows(head, core, counts, act, delta, far, weight, bias, held):
    width, dim, delta_width = weight.shape[1], act.shape[1], delta.shape[1]
    parts = [
        jax.ShapeDtypeStruct((tokens, dim), jnp.bfloat16)
        for tokens in (2 * WIN, WIN, WIN, WIN, WIN, WIN, WIN)
    ]
    return pl.pallas_call(
        far_kernel,
        in_specs=[SMEM] * 3 + [VMEM] * 3 + [ANYWHERE] * 3,
        out_specs=[ANYWHERE] * 7 + [VMEM] * 2,
        scratch_shapes=[
            pltpu.VMEM(bias.shape, bias.dtype),
            pltpu.VMEM((dim, width), jnp.float32),
            pltpu.VMEM((4, 2, ROW, dim), jnp.bfloat16),
            pltpu.VMEM((4, 2, ROW, width), jnp.bfloat16),
            pltpu.VMEM((4, 2, HALF, delta_width), jnp.bfloat16),
            pltpu.VMEM((4, 2 * WIN, dim), jnp.bfloat16),
            pltpu.SemaphoreType.DMA((4, 4)),
            pltpu.SemaphoreType.DMA((4, 2)),
        ],
        out_shape=parts
        + [jax.ShapeDtypeStruct((dim // 2, width), dtype) for dtype in (jnp.bfloat16, jnp.float32)],
        compiler_params=pltpu.CompilerParams(vmem_limit_bytes=LARGE_VMEM_BYTES),
        cost_estimate=COST,
        name="far_windows",
    )(
        head,
        core,
        counts,
        weight,
        bias,
        delta,
        act.reshape(WIN_ROWS, ROW, dim),
        far.reshape(WIN_ROWS, HALF, dim + delta_width),
        held.reshape(-1, WIN, width),
    )


def split_kernel(chip_ref, mine_ref, theirs_ref, own_ref, *outs):
    rows = own_ref.shape[0]
    for bits in range(4):
        at = pl.ds(pl.multiple_of((chip_ref[0] ^ bits) * rows, rows), rows)
        total = mine_ref[at, :] + theirs_ref[at, :].astype(jnp.float32)
        if bits:
            outs[bits - 1][...] = total.astype(jnp.bfloat16)
        else:
            own_ref[...] = total


def join_kernel(scale, chip_ref, own_ref, a_ref, b_ref, c_ref, out_ref):
    total = own_ref[...] + a_ref[...].astype(jnp.float32)
    total = (total + b_ref[...].astype(jnp.float32)) + c_ref[...].astype(jnp.float32)
    out_ref[...] = (total * scale).astype(jnp.bfloat16)


def gather_kernel(chip_ref, own_ref, a_ref, b_ref, c_ref, out_ref):
    rows = own_ref.shape[0]
    for bits, ref in enumerate((own_ref, a_ref, b_ref, c_ref)):
        out_ref[pl.ds(pl.multiple_of((chip_ref[0] ^ bits) * rows, rows), rows), :] = ref[...]


def widen_kernel(core_ref, mine_ref, theirs_ref, out_ref):
    rows = mine_ref.shape[0]
    for other, ref in enumerate((mine_ref, theirs_ref)):
        at = pl.ds(pl.multiple_of((core_ref[0] ^ other) * rows, rows), rows)
        out_ref[at, :] = ref[...].astype(jnp.float32)


def small(kernel, out_shape, place, *operands):
    vmem = pl.BlockSpec(memory_space=pltpu.VMEM)
    several = isinstance(out_shape, list)
    return pl.pallas_call(
        kernel,
        in_specs=[pl.BlockSpec(memory_space=pltpu.SMEM)] + [vmem] * len(operands),
        out_specs=[vmem] * len(out_shape) if several else vmem,
        out_shape=out_shape,
        compiler_params=pltpu.CompilerParams(vmem_limit_bytes=SMALL_VMEM_BYTES),
        cost_estimate=COST,
    )(place, *operands)


def after(x, *others):
    return lax.optimization_barrier((x, *others))[0]


def add(*parts):
    total = parts[0].astype(jnp.float32)
    for part in parts[1:]:
        total = total + part.astype(jnp.float32)
    return total.astype(jnp.bfloat16)


def line_shards(activations, qkv_weight, attn_grad, pos_bias, key_counts):
    dim, width = qkv_weight.shape
    total_tokens = activations.shape[0] * lax.axis_size("lon")
    head = lax.axis_index("head").reshape(1)
    lon = lax.axis_index("lon")
    core, chip = (lon % 2).reshape(1), (lon // 2).reshape(1)

    def hop(x, bits):
        return lax.ppermute(x, "head", [(i, i ^ bits) for i in range(lax.axis_size("head"))])

    far = passed_along(first_rows(activations, attn_grad), "lon", -1)
    here = (activations, attn_grad, qkv_weight, pos_bias)
    first, held = near_windows(0, 1, head, key_counts, *here, None)
    in_near = [hop(first, BESIDE)]
    *near, held = near_windows(1, 3, head, key_counts, *here, held)
    out_near = add(near[1], after(in_near[0], far))
    in_near.append(hop(after(near[0], out_near), BESIDE))
    in_near.append(hop(out_near, ACROSS))
    far = far.reshape(WIN_ROWS * HALF, far.shape[2])
    *parts, outgoing, mine = far_windows(
        head, core, key_counts, activations, attn_grad, far, qkv_weight, pos_bias, held
    )
    incoming = swapped(outgoing, 1)
    both_a, next_b, this_b, next_c, this_c, next_d, this_d = parts
    in_both, more_next = hop(both_a, BESIDE), hop(next_b, BESIDE)
    near_sum = add(near[2], *in_near[1:])

    block = (dim // 8, width)
    low = jax.ShapeDtypeStruct(block, jnp.bfloat16)
    own, *sent = small(
        split_kernel,
        [jax.ShapeDtypeStruct(block, jnp.float32), low, low, low],
        after(chip, near_sum),
        mine,
        incoming,
    )
    came = [swapped(part, 2 * (i + 1)) for i, part in enumerate(sent)]

    in_both = after(in_both, own, *came)
    out_next, out_this = add(next_c, in_both[:WIN]), add(this_c, in_both[WIN:])
    more_this = hop(after(this_b, out_next), BESIDE)
    over_next, over_this = hop(out_next, ACROSS), hop(out_this, ACROSS)

    scale = 1.0 / math.sqrt(total_tokens)
    done = small(functools.partial(join_kernel, scale), low, after(chip, out_this), own, *came)
    others = [swapped(done, 2 * (i + 1)) for i in range(3)]

    next_sum = last_sum(10_000_000_000, next_d, more_next, over_next)
    back = passed_along(next_sum, "lon", 1)
    half = jax.ShapeDtypeStruct((dim // 2, width), jnp.bfloat16)
    gathered = small(gather_kernel, half, chip, done, *others)
    other_half = swapped(gathered, 1)
    weight_grad = small(
        widen_kernel, jax.ShapeDtypeStruct((dim, width), jnp.float32), core, gathered, other_half
    )
    this_sum = last_sum(10_000_000_000, this_d, more_this, over_this)
    input_grad = jnp.concatenate(
        [x.reshape(2, -1, dim) for x in (after(back, weight_grad), near_sum, this_sum)], axis=1
    ).reshape(2 * ROW, dim)

    return (input_grad, weight_grad)


def sum_kernel(*refs):
    total = refs[0][...].astype(jnp.float32)
    for ref in refs[1:-1]:
        total = total + ref[...].astype(jnp.float32)
    refs[-1][...] = total.astype(refs[-1].dtype)


def last_sum(flops, *parts):
    return pl.pallas_call(
        sum_kernel,
        in_specs=[VMEM] * len(parts),
        out_specs=VMEM,
        out_shape=jax.ShapeDtypeStruct(parts[0].shape, parts[0].dtype),
        compiler_params=pltpu.CompilerParams(vmem_limit_bytes=SMALL_VMEM_BYTES),
        cost_estimate=pl.CostEstimate(flops=flops, bytes_accessed=1_000_000, transcendentals=0),
        name="last_sum",
    )(*parts)


def assemble(block_grid, far_rows):
    first_part = block_grid[:, :, 1]
    second_part = jnp.concatenate([block_grid[:, 1:, 0], far_rows[:, None]], axis=1)
    return jnp.concatenate([first_part, second_part], axis=2)


def window_grads(proj_win, delta_win, pos_bias, valid_count):
    scale_factor = 1.0 / math.sqrt(proj_win.shape[-1])
    queries = proj_win[:, :, :, 0]
    keys_part = proj_win[:, :, :, 1]
    values_part = proj_win[:, :, :, 2]
    scores = (
        jnp.einsum("nqhe,nkhe->nhqk", queries, keys_part, preferred_element_type=jnp.float32)
        * scale_factor
        + pos_bias[None]
    )
    positions = jnp.arange(proj_win.shape[1], dtype=jnp.int32)
    valid_keys = positions[None, :] < valid_count[:, None]
    scores = jnp.where(valid_keys[:, None, None, :], scores, -jnp.inf)
    row_max = jnp.max(scores, axis=-1, keepdims=True)
    weights = jnp.exp(scores - row_max)
    probs = weights / jnp.sum(weights, axis=-1, keepdims=True)
    grad_probs = jnp.einsum(
        "nqhe,nkhe->nhqk", delta_win, values_part, preferred_element_type=jnp.float32
    )
    grad_scores = probs * (grad_probs - jnp.sum(probs * grad_probs, axis=-1, keepdims=True))
    probs_low = probs.astype(jnp.bfloat16)
    grads_low = grad_scores.astype(jnp.bfloat16)
    grad_values = jnp.einsum(
        "nhqk,nqhe->nkhe", probs_low, delta_win, preferred_element_type=jnp.float32
    )
    grad_queries = (
        jnp.einsum("nhqk,nkhe->nqhe", grads_low, keys_part, preferred_element_type=jnp.float32)
        * scale_factor
    )
    grad_keys = (
        jnp.einsum("nhqk,nqhe->nkhe", grads_low, queries, preferred_element_type=jnp.float32)
        * scale_factor
    )
    return jnp.stack([grad_queries, grad_keys, grad_values], axis=3).astype(jnp.bfloat16)


def any_shards(activations, qkv_weight, attn_grad, pos_bias, key_counts):
    heads_here = pos_bias.shape[0]
    width_all = qkv_weight.shape[1]
    delta_width = attn_grad.shape[1]
    projected = jnp.dot(activations, qkv_weight, preferred_element_type=jnp.float32).astype(
        jnp.bfloat16
    )
    proj_grid = projected.reshape(WIN_ROWS, WIN_COLS, 2, HALF, width_all)
    delta_grid = attn_grad.reshape(WIN_ROWS, WIN_COLS, 2, HALF, delta_width)
    outgoing = jnp.concatenate([proj_grid[:, 0, 0], delta_grid[:, 0, 0]], axis=2)
    incoming = passed_along(outgoing, "lon", -1)
    proj_win = assemble(proj_grid, incoming[:, :, :width_all])
    delta_win = assemble(delta_grid, incoming[:, :, width_all:])
    gradients = window_grads(
        proj_win.reshape(WIN_ROWS * WIN_COLS, WIN, heads_here, 3, HEAD_DIM),
        delta_win.reshape(WIN_ROWS * WIN_COLS, WIN, heads_here, HEAD_DIM),
        pos_bias,
        key_counts,
    ).reshape(WIN_ROWS, WIN_COLS, WIN, width_all)
    leading = gradients[:, :, :HALF]
    trailing = gradients[:, :, HALF:]
    returned = passed_along(trailing[:, WIN_COLS - 1], "lon", 1)
    first_halves = jnp.concatenate([returned[:, None], trailing[:, : WIN_COLS - 1]], axis=1)
    grad_proj = jnp.stack([first_halves, leading], axis=2).reshape(BAND, width_all)
    local_grad = lax.dot_general(
        activations, grad_proj, (((0,), (0,)), ((), ())), preferred_element_type=jnp.float32
    )
    total_tokens = activations.shape[0] * lax.axis_size("lon")
    weight_grad = lax.psum(local_grad, "lon") / math.sqrt(total_tokens)
    partial_grad = lax.dot_general(
        grad_proj, qkv_weight, (((1,), (1,)), ((), ())), preferred_element_type=jnp.float32
    )
    partial_low = lax.optimization_barrier(partial_grad.astype(jnp.bfloat16)).astype(jnp.float32)
    input_grad = lax.psum_scatter(
        partial_low.astype(jnp.bfloat16), "head", scatter_dimension=0, tiled=True
    )
    return (input_grad, weight_grad)


def solution(mesh):
    placed = (P("lon", None), P(None, "head"), P("lon", "head"), P("head", None, None), P("lon"))
    on_line = mesh.shape["head"] == 4 and mesh.shape["lon"] == 8
    return jax.shard_map(
        line_shards if on_line else any_shards,
        mesh=mesh,
        in_specs=placed,
        out_specs=(P(("lon", "head"), None), P(None, "head")),
        check_vma=False,
    )
```

```python
import functools
import math

import jax
import jax.numpy as jnp
from jax import lax
from jax.experimental import pallas as pl
from jax.experimental.pallas import tpu as pltpu
from jax.sharding import PartitionSpec as P

HEAD_DIM = 64
WIN = 128
WIN_ROWS = 8
WIN_COLS = 2
HALF = WIN // 2
BAND = WIN_ROWS * WIN_COLS * WIN
ROW = WIN_COLS * WIN
NEAR_VMEM_BYTES = 48 * 1024 * 1024
LARGE_VMEM_BYTES = 56 * 1024 * 1024
HELD_ROWS = 12 * 1024
SMALL_VMEM_BYTES = 12 * 1024 * 1024

BESIDE, ACROSS = 1, 2
ORDER = (3, 1, 2, 0)
COST = pl.CostEstimate(flops=1_000_000, bytes_accessed=100_000, transcendentals=0)


def passed_along(shard, axis, by):
    size = lax.axis_size(axis)
    return lax.ppermute(shard, axis, [(i, (i + by) % size) for i in range(size)])


def swapped(shard, bits):
    size = lax.axis_size("lon")
    return lax.ppermute(shard, "lon", [(i, i ^ bits) for i in range(size)])


def attend(proj, delta, bias_ref, counts):
    scale = 1.0 / math.sqrt(HEAD_DIM)
    low = lax.broadcasted_iota(jnp.int32, (WIN, 2 * HEAD_DIM), 1) < HEAD_DIM
    key_at = lax.broadcasted_iota(jnp.int32, (WIN, WIN), 0)

    def both(pair):
        zero = jnp.zeros_like(pair)
        return jnp.concatenate([jnp.where(low, pair, zero), jnp.where(low, zero, pair)], axis=0)

    def rolled(x):
        return pltpu.roll(x, HEAD_DIM, 1)

    def dot(x, y, on):
        return lax.dot_general(x, y, (on, ((), ())), preferred_element_type=jnp.float32)

    pairs = proj.shape[1] // (6 * HEAD_DIM)
    units = [(w, p) for w in range(2) for p in range(pairs)]
    scored, softened, tiles = [], [], []
    for w, p in units:
        rows = slice(w * WIN, (w + 1) * WIN)
        at = [proj[rows, (3 * p + i) * WIN : (3 * p + i + 1) * WIN] for i in range(3)]
        queries = jnp.where(low, at[0], at[1]).astype(jnp.bfloat16)
        keys = rolled(jnp.where(low, at[2], at[0])).astype(jnp.bfloat16)
        values = jnp.where(low, at[1], at[2]).astype(jnp.bfloat16)
        grads = delta[rows, p * WIN : (p + 1) * WIN]
        two_keys = both(keys)
        scores = dot(two_keys, queries, ((1,), (1,)))
        grad_probs = dot(both(values), grads, ((1,), (1,)))
        scored.append((queries, two_keys, grads, scores, grad_probs))
    for (w, p), (queries, two_keys, grads, scores, grad_probs) in zip(units, scored):
        probs_low, grads_low = [], []
        for h in range(2):
            head = slice(h * WIN, (h + 1) * WIN)
            biased = scores[head] * scale + bias_ref[2 * p + h]
            biased = jnp.where(key_at < counts[w], biased, -jnp.inf)
            weights = jnp.exp(biased - jnp.max(biased, axis=0, keepdims=True))
            probs = weights * (1.0 / jnp.sum(weights, axis=0, keepdims=True))
            inner = jnp.sum(probs * grad_probs[head], axis=0, keepdims=True)
            probs_low.append(probs.astype(jnp.bfloat16))
            grads_low.append((probs * (grad_probs[head] - inner)).astype(jnp.bfloat16))
        softened.append((queries, two_keys, grads, probs_low, grads_low))
    for queries, two_keys, grads, probs_low, grads_low in softened:
        grad_values = dot(jnp.concatenate(probs_low, axis=1), both(grads), ((1,), (0,)))
        grad_keys = dot(jnp.concatenate(grads_low, axis=1), both(queries), ((1,), (0,)))
        grad_queries = dot(jnp.concatenate(grads_low, axis=0), two_keys, ((0,), (0,))) * scale
        grad_keys = rolled(grad_keys * scale)
        tiles.append(
            [
                jnp.where(low, grad_queries, grad_keys).astype(jnp.bfloat16),
                jnp.where(low, grad_values, grad_queries).astype(jnp.bfloat16),
                jnp.where(low, grad_keys, grad_values).astype(jnp.bfloat16),
            ]
        )
    return jnp.concatenate(
        [jnp.concatenate(sum(tiles[w * pairs : (w + 1) * pairs], []), axis=1) for w in range(2)],
        axis=0,
    )


def block_at(head, step):
    bits = jnp.where(step == 3, ORDER[3], ORDER[2])
    bits = jnp.where(step == 1, ORDER[1], bits)
    return head ^ jnp.where(step == 0, ORDER[0], bits)


def pack_kernel(act_ref, delta_ref, out_ref, sems):
    dim = act_ref.shape[2]
    copies = [
        pltpu.make_async_copy(
            act_ref.at[:, pl.ds(0, HALF), :], out_ref.at[:, :, pl.ds(0, dim)], sems.at[0]
        ),
        pltpu.make_async_copy(
            delta_ref.at[:, pl.ds(0, HALF), :],
            out_ref.at[:, :, pl.ds(dim, delta_ref.shape[2])],
            sems.at[1],
        ),
    ]
    for copy in copies:
        copy.start()
    for copy in copies:
        copy.wait()


def first_rows(act, delta):
    dim, delta_width = act.shape[1], delta.shape[1]
    anywhere = pl.BlockSpec(memory_space=pl.ANY)
    return pl.pallas_call(
        pack_kernel,
        in_specs=[anywhere, anywhere],
        out_specs=pl.BlockSpec(memory_space=pltpu.VMEM),
        out_shape=jax.ShapeDtypeStruct((WIN_ROWS, HALF, dim + delta_width), act.dtype),
        scratch_shapes=[pltpu.SemaphoreType.DMA((2,))],
        name="first_rows",
    )(act.reshape(WIN_ROWS, ROW, dim), delta.reshape(WIN_ROWS, ROW, delta_width))


def turned_biases(bias_ref, turned_ref):
    for h in range(bias_ref.shape[0]):
        turned_ref[h] = bias_ref[h].T


def counts_of(counts_ref, block, column):
    first = block * 2 * WIN_COLS + column
    return [counts_ref[first], counts_ref[first + WIN_COLS]]


def part_of(grads, weight):
    return lax.dot_general(
        grads, weight, (((1,), (1,)), ((), ())), preferred_element_type=jnp.float32
    ).astype(jnp.bfloat16)


def near_kernel(start, steps, head_ref, counts_ref, weight_ref, bias_ref, delta_ref, act_ref, *rest):
    *outs, held_ref = rest[-6 - steps : -5]
    turned_ref, rows_ref, parts_ref, grads_ref, sems = rest[-5:]
    tokens = 2 * WIN

    def fetch(k):
        block = block_at(head_ref[0], start + k)
        return pltpu.make_async_copy(
            act_ref.at[pl.ds(2 * block, 2), pl.ds(HALF, WIN), :], rows_ref.at[k], sems.at[2, k]
        )

    def put(k):
        held_rows = held_ref.at[pl.ds((start + k) * tokens, tokens), :]
        return [
            pltpu.make_async_copy(parts_ref.at[k], outs[k], sems.at[0, k]),
            pltpu.make_async_copy(grads_ref.at[k], held_rows, sems.at[1, k]),
        ]

    fetch(0).start()
    turned_biases(bias_ref, turned_ref)
    for k in range(steps):
        block = block_at(head_ref[0], start + k)
        base = pl.multiple_of(block * 2 * ROW, 2 * ROW)
        delta = [delta_ref[pl.ds(base + i * ROW + HALF, WIN), :] for i in range(2)]
        fetch(k).wait()
        if k + 1 < steps:
            fetch(k + 1).start()
        weight = weight_ref[...]
        rows = rows_ref[k].reshape(tokens, weight.shape[0])
        proj = jnp.dot(rows, weight, preferred_element_type=jnp.float32)
        counts = counts_of(counts_ref, block, 0)
        grads = attend(proj, jnp.concatenate(delta, axis=0), turned_ref, counts)
        grads_ref[k] = grads
        parts_ref[k] = part_of(grads, weight)
        for copy in put(k):
            copy.start()
    for k in range(steps):
        for copy in put(k):
            copy.wait()


VMEM = pl.BlockSpec(memory_space=pltpu.VMEM)
SMEM = pl.BlockSpec(memory_space=pltpu.SMEM)
ANYWHERE = pl.BlockSpec(memory_space=pl.ANY)


def near_windows(start, steps, head, counts, act, delta, weight, bias, held):
    width, dim = weight.shape[1], act.shape[1]
    tokens = 2 * WIN
    operands = [head, counts, weight, bias, delta, act.reshape(WIN_ROWS, ROW, dim)]
    specs = [SMEM, SMEM, VMEM, VMEM, VMEM, ANYWHERE]
    aliases = {}
    if held is not None:
        aliases = {len(operands): steps}
        operands.append(held)
        specs.append(ANYWHERE)
    part = jax.ShapeDtypeStruct((tokens, dim), jnp.bfloat16)
    return pl.pallas_call(
        functools.partial(near_kernel, start, steps),
        in_specs=specs,
        out_specs=[ANYWHERE] * (steps + 1),
        scratch_shapes=[
            pltpu.VMEM(bias.shape, bias.dtype),
            pltpu.VMEM((steps, 2, WIN, dim), jnp.bfloat16),
            pltpu.VMEM((steps, tokens, dim), jnp.bfloat16),
            pltpu.VMEM((steps, tokens, width), jnp.bfloat16),
            pltpu.SemaphoreType.DMA((3, steps)),
        ],
        out_shape=[part] * steps + [jax.ShapeDtypeStruct((HELD_ROWS, width), jnp.bfloat16)],
        input_output_aliases=aliases,
        compiler_params=pltpu.CompilerParams(vmem_limit_bytes=NEAR_VMEM_BYTES),
        cost_estimate=COST,
        name="near_windows",
    )(*operands)


def far_kernel(
    head_ref, core_ref, counts_ref, weight_ref, bias_ref, delta_ref, act_ref, far_ref, held_ref, *rest
):
    outs, send_ref, keep_ref, *scratch = rest[:7], *rest[7:]
    turned_ref, total_ref, rows_ref, grads_ref, halo_ref, parts_ref, in_sems, out_sems = scratch
    dim, delta_width = act_ref.shape[2], delta_ref.shape[1]

    def fetch(k):
        block = block_at(head_ref[0], k)
        copies = [
            (
                act_ref.at[pl.ds(2 * block, 2), pl.ds(HALF, ROW - HALF), :],
                rows_ref.at[k, :, pl.ds(0, ROW - HALF), :],
            ),
            (
                far_ref.at[pl.ds(2 * block, 2), :, pl.ds(0, dim)],
                rows_ref.at[k, :, pl.ds(ROW - HALF, HALF), :],
            ),
            (far_ref.at[pl.ds(2 * block, 2), :, pl.ds(dim, delta_width)], halo_ref.at[k]),
            (held_ref.at[pl.ds(2 * k, 2), :, :], grads_ref.at[k, :, pl.ds(0, WIN), :]),
        ]
        return [
            pltpu.make_async_copy(source, target, in_sems.at[k, i])
            for i, (source, target) in enumerate(copies)
        ]

    halves = [pl.ds(0, WIN), pl.ds(WIN, WIN)]
    put = [[pltpu.make_async_copy(parts_ref.at[0], outs[0], out_sems.at[0, 0])]]
    put += [
        [
            pltpu.make_async_copy(parts_ref.at[k, halves[j], :], outs[2 * k - 1 + j], out_sems.at[k, j])
            for j in range(2)
        ]
        for k in range(1, 4)
    ]
    for copy in fetch(0):
        copy.start()
    turned_biases(bias_ref, turned_ref)
    for k in range(4):
        block = block_at(head_ref[0], k)
        base = pl.multiple_of(block * 2 * ROW, 2 * ROW)
        for copy in fetch(k):
            copy.wait()
        if k < 3:
            for copy in fetch(k + 1):
                copy.start()
        delta = []
        for i in range(2):
            delta += [delta_ref[pl.ds(base + (i + 1) * ROW - HALF, HALF), :], halo_ref[k, i]]
        weight = weight_ref[...]
        rows = rows_ref[k, :, WIN:, :].reshape(2 * WIN, dim)
        proj = jnp.dot(rows, weight, preferred_element_type=jnp.float32)
        counts = counts_of(counts_ref, block, 1)
        grads = attend(proj, jnp.concatenate(delta, axis=0), turned_ref, counts)
        grads_ref[k, 0, WIN:, :] = grads[:WIN]
        grads_ref[k, 1, WIN:, :] = grads[WIN:]
        part = part_of(grads, weight)
        parts_ref[k, :HALF] = part[HALF:WIN]
        parts_ref[k, HALF:WIN] = part[WIN + HALF :]
        parts_ref[k, WIN : WIN + HALF] = part[:HALF]
        parts_ref[k, WIN + HALF :] = part[WIN : WIN + HALF]
        for copy in put[k]:
            copy.start()
        product = lax.dot_general(
            rows_ref[k].reshape(2 * ROW, dim),
            grads_ref[k].reshape(2 * ROW, weight.shape[1]),
            (((0,), (0,)), ((), ())),
            preferred_element_type=jnp.float32,
        )
        if k:
            total_ref[...] += product
        else:
            total_ref[...] = product
    half = dim // 2
    core = core_ref[0]
    send_ref[...] = total_ref[pl.ds(pl.multiple_of((1 - core) * half, half), half), :].astype(
        jnp.bfloat16
    )
    keep_ref[...] = total_ref[pl.ds(pl.multiple_of(core * half, half), half), :]
    for copy in sum(put, []):
        copy.wait()


def far_windows(head, core, counts, act, delta, far, weight, bias, held):
    width, dim, delta_width = weight.shape[1], act.shape[1], delta.shape[1]
    parts = [
        jax.ShapeDtypeStruct((tokens, dim), jnp.bfloat16)
        for tokens in (2 * WIN, WIN, WIN, WIN, WIN, WIN, WIN)
    ]
    return pl.pallas_call(
        far_kernel,
        in_specs=[SMEM] * 3 + [VMEM] * 3 + [ANYWHERE] * 3,
        out_specs=[ANYWHERE] * 7 + [VMEM] * 2,
        scratch_shapes=[
            pltpu.VMEM(bias.shape, bias.dtype),
            pltpu.VMEM((dim, width), jnp.float32),
            pltpu.VMEM((4, 2, ROW, dim), jnp.bfloat16),
            pltpu.VMEM((4, 2, ROW, width), jnp.bfloat16),
            pltpu.VMEM((4, 2, HALF, delta_width), jnp.bfloat16),
            pltpu.VMEM((4, 2 * WIN, dim), jnp.bfloat16),
            pltpu.SemaphoreType.DMA((4, 4)),
            pltpu.SemaphoreType.DMA((4, 2)),
        ],
        out_shape=parts
        + [jax.ShapeDtypeStruct((dim // 2, width), dtype) for dtype in (jnp.bfloat16, jnp.float32)],
        compiler_params=pltpu.CompilerParams(vmem_limit_bytes=LARGE_VMEM_BYTES),
        cost_estimate=COST,
        name="far_windows",
    )(
        head,
        core,
        counts,
        weight,
        bias,
        delta,
        act.reshape(WIN_ROWS, ROW, dim),
        far.reshape(WIN_ROWS, HALF, dim + delta_width),
        held.reshape(-1, WIN, width),
    )


def split_kernel(chip_ref, mine_ref, theirs_ref, own_ref, *outs):
    rows = own_ref.shape[0]
    for bits in range(4):
        at = pl.ds(pl.multiple_of((chip_ref[0] ^ bits) * rows, rows), rows)
        total = mine_ref[at, :] + theirs_ref[at, :].astype(jnp.float32)
        if bits:
            outs[bits - 1][...] = total.astype(jnp.bfloat16)
        else:
            own_ref[...] = total


def join_kernel(scale, chip_ref, own_ref, a_ref, b_ref, c_ref, out_ref):
    total = own_ref[...] + a_ref[...].astype(jnp.float32)
    total = (total + b_ref[...].astype(jnp.float32)) + c_ref[...].astype(jnp.float32)
    out_ref[...] = (total * scale).astype(jnp.bfloat16)


def gather_kernel(chip_ref, own_ref, a_ref, b_ref, c_ref, out_ref):
    rows = own_ref.shape[0]
    for bits, ref in enumerate((own_ref, a_ref, b_ref, c_ref)):
        out_ref[pl.ds(pl.multiple_of((chip_ref[0] ^ bits) * rows, rows), rows), :] = ref[...]


def widen_kernel(core_ref, mine_ref, theirs_ref, out_ref):
    rows = mine_ref.shape[0]
    for other, ref in enumerate((mine_ref, theirs_ref)):
        at = pl.ds(pl.multiple_of((core_ref[0] ^ other) * rows, rows), rows)
        out_ref[at, :] = ref[...].astype(jnp.float32)


def small(kernel, out_shape, place, *operands):
    vmem = pl.BlockSpec(memory_space=pltpu.VMEM)
    several = isinstance(out_shape, list)
    return pl.pallas_call(
        kernel,
        in_specs=[pl.BlockSpec(memory_space=pltpu.SMEM)] + [vmem] * len(operands),
        out_specs=[vmem] * len(out_shape) if several else vmem,
        out_shape=out_shape,
        compiler_params=pltpu.CompilerParams(vmem_limit_bytes=SMALL_VMEM_BYTES),
        cost_estimate=COST,
    )(place, *operands)


def after(x, *others):
    return lax.optimization_barrier((x, *others))[0]


def add(*parts):
    total = parts[0].astype(jnp.float32)
    for part in parts[1:]:
        total = total + part.astype(jnp.float32)
    return total.astype(jnp.bfloat16)


def line_shards(activations, qkv_weight, attn_grad, pos_bias, key_counts):
    dim, width = qkv_weight.shape
    total_tokens = activations.shape[0] * lax.axis_size("lon")
    head = lax.axis_index("head").reshape(1)
    lon = lax.axis_index("lon")
    core, chip = (lon % 2).reshape(1), (lon // 2).reshape(1)

    def hop(x, bits):
        return lax.ppermute(x, "head", [(i, i ^ bits) for i in range(lax.axis_size("head"))])

    far = passed_along(first_rows(activations, attn_grad), "lon", -1)
    here = (activations, attn_grad, qkv_weight, pos_bias)
    first, held = near_windows(0, 1, head, key_counts, *here, None)
    in_near = [hop(first, BESIDE)]
    *near, held = near_windows(1, 3, head, key_counts, *here, held)
    out_near = add(near[1], after(in_near[0], far))
    in_near.append(hop(after(near[0], out_near), BESIDE))
    in_near.append(hop(out_near, ACROSS))
    far = far.reshape(WIN_ROWS * HALF, far.shape[2])
    *parts, outgoing, mine = far_windows(
        head, core, key_counts, activations, attn_grad, far, qkv_weight, pos_bias, held
    )
    incoming = swapped(outgoing, 1)
    both_a, next_b, this_b, next_c, this_c, next_d, this_d = parts
    in_both, more_next = hop(both_a, BESIDE), hop(next_b, BESIDE)
    near_sum = add(near[2], *in_near[1:])

    block = (dim // 8, width)
    low = jax.ShapeDtypeStruct(block, jnp.bfloat16)
    own, *sent = small(
        split_kernel,
        [jax.ShapeDtypeStruct(block, jnp.float32), low, low, low],
        after(chip, near_sum),
        mine,
        incoming,
    )
    came = [swapped(part, 2 * (i + 1)) for i, part in enumerate(sent)]

    in_both = after(in_both, own, came[0])
    out_next, out_this = both_sums(next_c, this_c, in_both)
    more_this = hop(after(this_b, out_next), BESIDE)
    over_next, over_this = hop(out_next, ACROSS), hop(out_this, ACROSS)

    scale = 1.0 / math.sqrt(total_tokens)
    done = small(functools.partial(join_kernel, scale), low, after(chip, out_this), own, *came)
    others = [swapped(done, 2 * (i + 1)) for i in range(3)]

    next_sum = last_sum(10_000_000_000, next_d, more_next, over_next)
    back = passed_along(next_sum, "lon", 1)
    half = jax.ShapeDtypeStruct((dim // 2, width), jnp.bfloat16)
    gathered = small(gather_kernel, half, chip, done, *others)
    other_half = swapped(gathered, 1)
    weight_grad = small(
        widen_kernel, jax.ShapeDtypeStruct((dim, width), jnp.float32), core, gathered, other_half
    )
    this_sum = last_sum(10_000_000_000, this_d, more_this, over_this)
    input_grad = jnp.concatenate(
        [x.reshape(2, -1, dim) for x in (after(back, weight_grad), near_sum, this_sum)], axis=1
    ).reshape(2 * ROW, dim)

    return (input_grad, weight_grad)


def sum_kernel(*refs):
    total = refs[0][...].astype(jnp.float32)
    for ref in refs[1:-1]:
        total = total + ref[...].astype(jnp.float32)
    refs[-1][...] = total.astype(refs[-1].dtype)


def both_kernel(next_ref, this_ref, came_ref, out_next_ref, out_this_ref):
    came = came_ref[...].astype(jnp.float32)
    out_next_ref[...] = (next_ref[...].astype(jnp.float32) + came[:WIN]).astype(out_next_ref.dtype)
    out_this_ref[...] = (this_ref[...].astype(jnp.float32) + came[WIN:]).astype(out_this_ref.dtype)


def both_sums(next_part, this_part, came):
    shape = jax.ShapeDtypeStruct(next_part.shape, next_part.dtype)
    return pl.pallas_call(
        both_kernel,
        in_specs=[VMEM] * 3,
        out_specs=[VMEM] * 2,
        out_shape=[shape, shape],
        compiler_params=pltpu.CompilerParams(vmem_limit_bytes=SMALL_VMEM_BYTES),
        cost_estimate=pl.CostEstimate(flops=1_000_000_000, bytes_accessed=1_000_000, transcendentals=0),
        name="both_sums",
    )(next_part, this_part, came)


def last_sum(flops, *parts):
    return pl.pallas_call(
        sum_kernel,
        in_specs=[VMEM] * len(parts),
        out_specs=VMEM,
        out_shape=jax.ShapeDtypeStruct(parts[0].shape, parts[0].dtype),
        compiler_params=pltpu.CompilerParams(vmem_limit_bytes=SMALL_VMEM_BYTES),
        cost_estimate=pl.CostEstimate(flops=flops, bytes_accessed=1_000_000, transcendentals=0),
        name="last_sum",
    )(*parts)


def assemble(block_grid, far_rows):
    first_part = block_grid[:, :, 1]
    second_part = jnp.concatenate([block_grid[:, 1:, 0], far_rows[:, None]], axis=1)
    return jnp.concatenate([first_part, second_part], axis=2)


def window_grads(proj_win, delta_win, pos_bias, valid_count):
    scale_factor = 1.0 / math.sqrt(proj_win.shape[-1])
    queries = proj_win[:, :, :, 0]
    keys_part = proj_win[:, :, :, 1]
    values_part = proj_win[:, :, :, 2]
    scores = (
        jnp.einsum("nqhe,nkhe->nhqk", queries, keys_part, preferred_element_type=jnp.float32)
        * scale_factor
        + pos_bias[None]
    )
    positions = jnp.arange(proj_win.shape[1], dtype=jnp.int32)
    valid_keys = positions[None, :] < valid_count[:, None]
    scores = jnp.where(valid_keys[:, None, None, :], scores, -jnp.inf)
    row_max = jnp.max(scores, axis=-1, keepdims=True)
    weights = jnp.exp(scores - row_max)
    probs = weights / jnp.sum(weights, axis=-1, keepdims=True)
    grad_probs = jnp.einsum(
        "nqhe,nkhe->nhqk", delta_win, values_part, preferred_element_type=jnp.float32
    )
    grad_scores = probs * (grad_probs - jnp.sum(probs * grad_probs, axis=-1, keepdims=True))
    probs_low = probs.astype(jnp.bfloat16)
    grads_low = grad_scores.astype(jnp.bfloat16)
    grad_values = jnp.einsum(
        "nhqk,nqhe->nkhe", probs_low, delta_win, preferred_element_type=jnp.float32
    )
    grad_queries = (
        jnp.einsum("nhqk,nkhe->nqhe", grads_low, keys_part, preferred_element_type=jnp.float32)
        * scale_factor
    )
    grad_keys = (
        jnp.einsum("nhqk,nqhe->nkhe", grads_low, queries, preferred_element_type=jnp.float32)
        * scale_factor
    )
    return jnp.stack([grad_queries, grad_keys, grad_values], axis=3).astype(jnp.bfloat16)


def any_shards(activations, qkv_weight, attn_grad, pos_bias, key_counts):
    heads_here = pos_bias.shape[0]
    width_all = qkv_weight.shape[1]
    delta_width = attn_grad.shape[1]
    projected = jnp.dot(activations, qkv_weight, preferred_element_type=jnp.float32).astype(
        jnp.bfloat16
    )
    proj_grid = projected.reshape(WIN_ROWS, WIN_COLS, 2, HALF, width_all)
    delta_grid = attn_grad.reshape(WIN_ROWS, WIN_COLS, 2, HALF, delta_width)
    outgoing = jnp.concatenate([proj_grid[:, 0, 0], delta_grid[:, 0, 0]], axis=2)
    incoming = passed_along(outgoing, "lon", -1)
    proj_win = assemble(proj_grid, incoming[:, :, :width_all])
    delta_win = assemble(delta_grid, incoming[:, :, width_all:])
    gradients = window_grads(
        proj_win.reshape(WIN_ROWS * WIN_COLS, WIN, heads_here, 3, HEAD_DIM),
        delta_win.reshape(WIN_ROWS * WIN_COLS, WIN, heads_here, HEAD_DIM),
        pos_bias,
        key_counts,
    ).reshape(WIN_ROWS, WIN_COLS, WIN, width_all)
    leading = gradients[:, :, :HALF]
    trailing = gradients[:, :, HALF:]
    returned = passed_along(trailing[:, WIN_COLS - 1], "lon", 1)
    first_halves = jnp.concatenate([returned[:, None], trailing[:, : WIN_COLS - 1]], axis=1)
    grad_proj = jnp.stack([first_halves, leading], axis=2).reshape(BAND, width_all)
    local_grad = lax.dot_general(
        activations, grad_proj, (((0,), (0,)), ((), ())), preferred_element_type=jnp.float32
    )
    total_tokens = activations.shape[0] * lax.axis_size("lon")
    weight_grad = lax.psum(local_grad, "lon") / math.sqrt(total_tokens)
    partial_grad = lax.dot_general(
        grad_proj, qkv_weight, (((1,), (1,)), ((), ())), preferred_element_type=jnp.float32
    )
    partial_low = lax.optimization_barrier(partial_grad.astype(jnp.bfloat16)).astype(jnp.float32)
    input_grad = lax.psum_scatter(
        partial_low.astype(jnp.bfloat16), "head", scatter_dimension=0, tiled=True
    )
    return (input_grad, weight_grad)


def solution(mesh):
    placed = (P("lon", None), P(None, "head"), P("lon", "head"), P("head", None, None), P("lon"))
    on_line = mesh.shape["head"] == 4 and mesh.shape["lon"] == 8
    return jax.shard_map(
        line_shards if on_line else any_shards,
        mesh=mesh,
        in_specs=placed,
        out_specs=(P(("lon", "head"), None), P(None, "head")),
        check_vma=False,
    )
```
